32 devices in a mesh: groups: 1, vocab: 4 (over z), tokens: 4 (over y, x), sub: 2 (over core).
Axes of the slice: x: 2, y: 2, z: 4, core: 2. Of those that a mesh axis runs over, the one named last changes fastest.
Arguments:
- student_hidden: bfloat16 [32, 3072], P(('groups', 'vocab', 'tokens', 'sub')), may hold values from -41 to 41
- teacher_hidden: bfloat16 [32, 4096], P(('groups', 'vocab', 'tokens', 'sub')), may hold values from -41 to 41
- student_head: bfloat16 [3072, 8192], P(None, ('vocab', 'tokens', 'sub')), may hold values from -0.25 to 0.25
- teacher_head: bfloat16 [4096, 8192], P(None, ('vocab', 'tokens', 'sub')), may hold values from -0.1875 to 0.1875
- proposed_block: int32 [32, 32], P(('groups', 'vocab', 'tokens', 'sub')), may hold values from 0 to 63, all different within a row; in each aligned block of 32 rows (0 to 31, 32 to 63, ...) at most 32 rows name the same one
- proposed_offset: int32 [32, 32], P(('groups', 'vocab', 'tokens', 'sub')), may hold values from 0 to 127
Outputs:
- token_loss: float32 [32], P(('groups', 'vocab', 'tokens', 'sub'))
- student_grad: bfloat16 [32, 3072], P(('groups', 'vocab', 'tokens', 'sub'))
The draws below stay inside these ranges and needn't reach their ends.
Inputs may be any that keep to these rules, and one draw needn't show every extreme that they name: `proposed_block`: each token names 32 different blocks; within one replica no block is named by more than 32 tokens, and some block by exactly 32.
All inputs are finite; a program needn't handle non-finite values.
Results may differ from the reference program's by a relative error of at most 0.014.
Values may be sent and summed in bfloat16 or wider, within the bound.
A program may use at most 64 MiB of HBM per device.

```python
import math
import jax
import jax.numpy as jnp
import numpy as np
from jax import lax

DS = 3072
DT = 4096
VS = 256
BLK = 128
K = 32
SHARDS = 32
TOKENS = 32
VOCAB = 8192
BLOCKS = 64
CAP = 32


def draw_student_hidden(key, part):
    key = jax.random.fold_in(key, 11)
    value_key = jax.random.fold_in(key, 0)
    values = jnp.clip(jax.random.normal(value_key, (TOKENS, DS), jnp.float32), -5.0, 5.0)
    return values.astype(jnp.bfloat16)


def draw_teacher_hidden(key, part):
    key = jax.random.fold_in(key, 13)
    value_key = jax.random.fold_in(key, 0)
    values = jnp.clip(jax.random.normal(value_key, (TOKENS, DT), jnp.float32), -5.0, 5.0)
    return values.astype(jnp.bfloat16)


def set_ends(array, stream_key, smallest, largest):
    longest = array.shape.index(max(array.shape))
    spots = []
    for shift in (0, 1):
        where = [jax.random.randint(jax.random.fold_in(stream_key, axis), (), 0, length) for axis, length in enumerate(array.shape)]
        where[longest] = (where[longest] + shift) % array.shape[longest]
        spots.append(tuple(where))
    return array.at[spots[0]].set(smallest).at[spots[1]].set(largest)


def block_scale(stream_key, dims, shards, least, high):
    factor_of = 1.0
    for axis_at, parts in shards:
        steps = jax.random.uniform(jax.random.fold_in(jax.random.fold_in(stream_key, 6), axis_at), (parts,), jnp.float32, least / len(shards), high / len(shards))
        factor_of = factor_of * jnp.repeat(jnp.exp(steps), dims[axis_at] // parts).reshape((-1,) + (1,) * (len(dims) - 1 - axis_at))
    return factor_of


def deal_out(key, own, number, rows, amount, top, limit, slope):
    ranking = jax.random.permutation(key, amount)
    packed, ordinary = portions_of(amount, rows * top, limit, slope, True), portions_of(amount, rows * top, limit, slope, False)
    places = jnp.arange(amount)

    def named(lengths, offset_by):
        used = int((lengths > 0).sum())
        fixed = max(1, used // 4)
        passed = fixed + (places - fixed + offset_by * (used - fixed)) % max(1, amount - fixed)
        return jnp.zeros((amount,), jnp.int32).at[ranking[jnp.where(places < fixed, places, passed)]].set(jnp.asarray(lengths, jnp.int32))

    lengths = jnp.where(number % 4 == 0, named(packed, number // 4), named(ordinary, number - number // 4 - 1))
    mixed = jax.random.permutation(jax.random.fold_in(own, 3), amount)
    source_of, receiver = mixed[0:amount // 2 * 2:2], mixed[1:amount // 2 * 2:2]
    slack = jnp.minimum(lengths[source_of] - 1, limit - lengths[receiver]) // 2
    slack = jnp.where((source_of == ranking[0]) | (receiver == ranking[0]) | (lengths[receiver] == 0), 0, jnp.maximum(slack, 0))
    passed = jax.random.randint(jax.random.fold_in(own, 4), (amount // 2,), 0, 1 << 20) % (slack + 1)
    lengths = lengths.at[source_of].add(-passed).at[receiver].add(passed)
    items = jnp.searchsorted(jnp.cumsum(lengths), jnp.arange(rows * top), side="right").astype(jnp.int32)
    grid = items.reshape(top, rows).T
    grid = grid[jax.random.permutation(jax.random.fold_in(own, 1), rows)]
    offset_by = jax.random.randint(jax.random.fold_in(own, 2), (rows, 1), 0, top)
    return jnp.take_along_axis(grid, (jnp.arange(top)[None, :] + offset_by) % top, axis=1)


def portions_of(number_of, total, bound, slope, full):
    weights = [(1 << 20) // math.isqrt(grade ** slope) + 1 for grade in range(1, number_of + 1)]
    largest = bound if full else min(bound, max(-(-total // number_of), total * weights[0] // sum(weights)))
    least = 1 if total - largest >= number_of - 1 else 0
    given, surplus = [largest] + [least] * (number_of - 1), total - largest - least * (number_of - 1)
    while surplus > 0:
        movable = [i for i in range(1, number_of) if given[i] < largest] or [i for i in range(1, number_of) if given[i] < bound]
        pool, remaining = sum([weights[i] for i in movable]), surplus
        for i in movable:
            addition = min(bound - given[i], max(1, remaining * weights[i] // pool), surplus)
            given[i] = given[i] + addition
            surplus = surplus - addition
    return np.array(given)


def noise(own_key, extent, width, limit, pieces=(), kind=jnp.bfloat16):
    drawn = jax.random.normal(own_key, extent, jnp.float32) * width
    if len(pieces) > 0:
        drawn = block_scale(own_key, extent, pieces, -0.22, 0.18) * drawn
    return jnp.clip(drawn, min=-limit, max=limit).astype(kind)


def setup_inputs(seed: int = 0, part: int = 0) -> dict:
    key_of = jax.random.split(jax.random.key(seed), 7)
    own_keys = jax.random.split(jax.random.fold_in(key_of[6], part), 7)
    student_hidden = draw_student_hidden(jax.random.fold_in(jax.random.fold_in(key_of[6], part), 71), part)
    teacher_hidden = draw_teacher_hidden(jax.random.fold_in(jax.random.fold_in(key_of[6], part), 71), part)
    student_head = noise(key_of[2], (DS, VOCAB), (DS // 6) ** -0.5, 0.25, ((1, 32),))
    teacher_head = noise(key_of[3], (DT, VOCAB), (DT // 4) ** -0.5, 0.1875, ((1, 32),))
    proposed_block_keys = jax.random.split(jax.random.fold_in(own_keys[4], 1), TOKENS // TOKENS)
    proposed_block_turns = jax.random.permutation(jax.random.fold_in(own_keys[4], 3), TOKENS // TOKENS)
    proposed_block = jax.vmap(lambda own, number: deal_out(jax.random.fold_in(own_keys[4], 2), own, number, TOKENS, BLOCKS, K, CAP, 2))(proposed_block_keys, proposed_block_turns).reshape((TOKENS, K))
    proposed_offset = set_ends(jax.random.randint(own_keys[5], (TOKENS, K), 0, BLK), jax.random.fold_in(own_keys[5], 1), 0, BLK - 1).astype(jnp.int32)
    return {"student_hidden": student_hidden, "teacher_hidden": teacher_hidden, "student_head": student_head, "teacher_head": teacher_head, "proposed_block": proposed_block, "proposed_offset": proposed_offset}


mix_weight = 0.1
loss_scale = 64.0


def loss_terms(student_at, teacher_at, student_norm, teacher_norm):
    student_logprob = student_at - student_norm[:, None]
    teacher_logprob = teacher_at - teacher_norm[:, None]
    shifted = jnp.exp(student_at - jnp.max(student_at, axis=1, keepdims=True))
    weights = shifted / jnp.sum(shifted, axis=1, keepdims=True)
    mixture = jnp.logaddexp(student_logprob + math.log(mix_weight), teacher_logprob + math.log(1.0 - mix_weight))
    excess = student_logprob - mixture
    token_loss = jnp.sum(weights * excess, axis=1)
    mix_share = jnp.exp(student_logprob + math.log(mix_weight) - mixture)
    direct = weights * (1.0 - mix_share)
    grad_at = loss_scale * (weights * (excess - token_loss[:, None]) + direct)
    grad_mass = loss_scale * jnp.sum(direct, axis=1)
    return token_loss, grad_at, grad_mass


def reference(student_hidden, teacher_hidden, student_head, teacher_head, proposed_block, proposed_offset):
    token_iota = jnp.arange(TOKENS, dtype=jnp.int32)
    token_ids = (proposed_block * BLK + proposed_offset).astype(jnp.int32)
    student_logits = jnp.dot(student_hidden, student_head, preferred_element_type=jnp.float32)
    student_peak = jnp.max(student_logits, axis=1)
    student_norm = student_peak + jnp.log(jnp.sum(jnp.exp(student_logits - student_peak[:, None]), axis=1))
    teacher_logits = jnp.dot(teacher_hidden, teacher_head, preferred_element_type=jnp.float32)
    touched = jnp.zeros((TOKENS, BLOCKS), jnp.int32).at[token_iota[:, None], proposed_block].set(1) > 0
    col_mask = jnp.repeat(touched, BLK, axis=1)
    teacher_peak = jnp.max(jnp.where(col_mask, teacher_logits, -1e30), axis=1)
    teacher_norm = teacher_peak + jnp.log(jnp.sum(jnp.exp(jnp.where(col_mask, teacher_logits - teacher_peak[:, None], -1e30)), axis=1))
    student_at = jnp.take_along_axis(student_logits, token_ids, axis=1)
    teacher_at = jnp.take_along_axis(teacher_logits, token_ids, axis=1)
    token_loss, grad_at, grad_mass = loss_terms(student_at, teacher_at, student_norm, teacher_norm)
    logit_grad = -grad_mass[:, None] * jnp.exp(student_logits - student_norm[:, None])
    logit_grad = logit_grad.at[token_iota[:, None], token_ids].add(grad_at)
    grad_narrow = logit_grad.astype(jnp.bfloat16)

    def add_group(running, group):
        columns = lax.dynamic_slice_in_dim(grad_narrow, group * VS, VS, 1)
        head_cols = lax.dynamic_slice_in_dim(student_head, group * VS, VS, 1)
        product = lax.dot_general(columns, head_cols, (((1,), (1,)), ((), ())), preferred_element_type=jnp.float32)
        rounded = lax.optimization_barrier(product.astype(jnp.bfloat16))
        return running + rounded.astype(jnp.float32), None

    summed = lax.scan(add_group, jnp.zeros((TOKENS, DS), jnp.float32), jnp.arange(SHARDS, dtype=jnp.int32))[0]
    return token_loss, summed.astype(jnp.bfloat16)
```

```python
import functools
import math

import jax
import jax.numpy as jnp
from jax import lax
from jax.experimental import pallas as pl
from jax.experimental.pallas import tpu as pltpu
from jax.sharding import PartitionSpec as P

BLK = 128
LANES = 128
NONE = -1e30
AXES = ("vocab", "tokens", "sub")
mix_weight = 0.1
loss_scale = 64.0
MESH = pl.DeviceIdType.MESH


def loss_planes(at, student_max, student_sum, teacher_max, teacher_sum):
    top = lambda x: jnp.max(x, axis=0, keepdims=True)
    add = lambda x: jnp.sum(x, axis=0, keepdims=True)
    peak = top(student_max)
    student_norm = peak + jnp.log(add(student_sum * jnp.exp(student_max - peak)))
    teacher_peak = top(teacher_max)
    teacher_norm = teacher_peak + jnp.log(add(teacher_sum * jnp.exp(teacher_max - teacher_peak)))
    at_peak = functools.reduce(jnp.maximum, [top(s) for s, _ in at])
    shifted = [jnp.exp(s - at_peak) for s, _ in at]
    scale = 1.0 / sum(add(x) for x in shifted)
    weights = [x * scale for x in shifted]
    excess, direct = [], []
    for (student, teacher), weight in zip(at, weights):
        a = student - student_norm + math.log(mix_weight)
        b = teacher - teacher_norm + math.log(1.0 - mix_weight)
        mixture = jnp.maximum(a, b) + jnp.log(1.0 + jnp.exp(-jnp.abs(a - b)))
        excess.append(student - student_norm - mixture)
        direct.append(weight * (1.0 - jnp.exp(a - mixture)))
    token_loss = sum(add(w * e) for w, e in zip(weights, excess))
    grad_at = [loss_scale * (w * (e - token_loss) + d) for w, e, d in zip(weights, excess, direct)]
    mass = loss_scale * sum(add(d) for d in direct)
    return token_loss, grad_at, mass, student_norm


def kernel(
    sizes, sh_hbm, th_hbm, ws_hbm, wt_hbm, blk_hbm, off_hbm, loss_ref, grad_ref,
    sh, th, ws, wt, blk, off, stage, gbuf, xs, sbuf, ps, pbuf, rbuf,
    load_sem, gz_sem, gx_sem, gc_sem, gr_sem, ss_sem, sr_sem, ps_sem, pr_sem,
):
    V, T, S = sizes
    n = V * T * S
    g = lax.axis_index("groups")
    v, t, s = (lax.axis_index(a) for a in AXES)
    me = (v * T + t) * S + s
    ds_rows, dt_rows = sh.shape[1] // LANES, th.shape[1] // LANES
    rows = gbuf.shape[1]

    def device(p):
        return (g, p // (T * S), (p // S) % T, p % S)

    def slot(a, b, c):
        return (a * T + b) * S + c

    loads = [
        pltpu.make_async_copy(src, dst, load_sem.at[i])
        for i, (src, dst) in enumerate(
            [(sh_hbm, sh), (th_hbm, th), (blk_hbm, blk), (off_hbm, off), (ws_hbm, ws), (wt_hbm, wt)]
        )
    ]
    for load in loads:
        load.start()

    barrier = pltpu.get_barrier_semaphore()

    @pl.loop(1, n)
    def _(i):
        pl.semaphore_signal(barrier, inc=1, device_id=device(lax.rem(me + i, n)), device_id_type=MESH)

    for load in loads[:4]:
        load.wait()

    for j in range(ds_rows):
        stage[j : j + 1, :] = sh[:, j * LANES : (j + 1) * LANES].astype(jnp.float32)
    for j in range(dt_rows):
        stage[ds_rows + j : ds_rows + j + 1, :] = th[:, j * LANES : (j + 1) * LANES].astype(jnp.float32)
    K = blk.shape[1]
    base = ds_rows + dt_rows
    stage[base : base + 8, :] = jnp.zeros((8, LANES), jnp.float32)
    block_row = blk[...]
    stage[base : base + 1, :K] = (block_row // 64).astype(jnp.float32)
    stage[base + 1 : base + 2, :K] = (block_row % 64).astype(jnp.float32)
    stage[base + 2 : base + 3, :K] = off[...].astype(jnp.float32)
    gbuf[me] = stage[...].astype(jnp.bfloat16)

    pl.semaphore_wait(barrier, n - 1)

    def send(at, to, sem):
        return pltpu.make_async_remote_copy(
            src_ref=gbuf.at[at], dst_ref=gbuf.at[at], send_sem=sem, recv_sem=gr_sem.at[at],
            device_id=to, device_id_type=MESH,
        )

    other = lax.rem(s + 1, S)

    def to_z(d):
        return send(me, (g, lax.rem(v + d, V), t, s), gz_sem.at[d])

    def to_xy(a, d):
        return send(slot(a, t, s), (g, v, lax.rem(t + d, T), s), gx_sem.at[a, d])

    def to_core(a, b):
        return send(slot(a, b, s), (g, v, t, other), gc_sem.at[a, b])

    def unpack(at):
        xs[pl.ds(at, rows, stride=n), :] = gbuf[at].astype(jnp.float32)

    @pl.loop(1, V)
    def _(d):
        to_z(d).start()

    for d in range(1, T):
        to_xy(v, d).start()
    to_core(v, t).start()
    unpack(me)

    @pl.loop(1, V)
    def _(d):
        a = lax.rem(v + V - d, V)
        send(slot(a, t, s), (g, v, t, other), gc_sem.at[a, t]).wait_recv()
        for e in range(1, T):
            to_xy(a, e).start()
        to_core(a, t).start()
        unpack(slot(a, t, s))

    @pl.loop(0, V)
    def _(d):
        a = lax.rem(v + V - d, V)
        for e in range(1, T):
            b = lax.rem(t + T - e, T)
            to_core(a, b).wait_recv()
            to_core(a, b).start()
            unpack(slot(a, b, s))

    @pl.loop(0, V)
    def _(d):
        a = lax.rem(v + V - d, V)
        for e in range(T):
            b = lax.rem(t + T - e, T)
            at = slot(a, b, other)
            send(at, (g, v, t, other), gc_sem.at[a, b]).wait_recv()
            unpack(at)

    def chunks(lo, hi):
        return jnp.concatenate([xs[c * n : (c + 1) * n, :] for c in range(lo, hi)], axis=1).astype(jnp.bfloat16)

    loads[4].wait()
    student = jnp.dot(chunks(0, ds_rows), ws[...], preferred_element_type=jnp.float32)
    loads[5].wait()
    teacher = jnp.dot(chunks(ds_rows, base), wt[...], preferred_element_type=jnp.float32)

    col_width = ws.shape[1]
    here = col_width // BLK
    block_all = xs[base * n : (base + 1) * n, :] * 64.0 + xs[(base + 1) * n : (base + 2) * n, :]
    offset_all = xs[(base + 2) * n : (base + 3) * n, :] + 1.0
    lane = lax.broadcasted_iota(jnp.int32, (n, LANES), 1)
    student_at, teacher_at, hits, masked = [], [], [], []
    for b in range(here):
        wanted = (me * here + b).astype(jnp.float32)
        chosen = jnp.where((block_all == wanted) & (lane < K), offset_all, 0.0)
        offset = jnp.sum(chosen, axis=1, keepdims=True)
        named = offset > 0.0
        hit = lane.astype(jnp.float32) + 1.0 == offset
        part = slice(b * BLK, (b + 1) * BLK)
        at_s = jnp.sum(jnp.where(hit, student[:, part], 0.0), axis=1, keepdims=True)
        student_at.append(jnp.where(named, at_s, NONE))
        teacher_at.append(jnp.sum(jnp.where(hit, teacher[:, part], 0.0), axis=1, keepdims=True))
        hits.append(hit)
        masked.append(jnp.where(named, teacher[:, part], NONE))
    teacher_seen = jnp.concatenate(masked, axis=1)
    student_max = jnp.max(student, axis=1, keepdims=True)
    student_sum = jnp.sum(jnp.exp(student - student_max), axis=1, keepdims=True)
    teacher_max = jnp.max(teacher_seen, axis=1, keepdims=True)
    teacher_sum = jnp.sum(
        jnp.where(teacher_seen > 0.5 * NONE, jnp.exp(teacher_seen - teacher_max), 0.0), axis=1, keepdims=True
    )
    values = student_at + teacher_at + [student_max, student_sum, teacher_max, teacher_sum]

    span = min(n, LANES)
    per = LANES // span
    planes = n // span
    width = len(values) // per
    wide = lax.broadcasted_iota(jnp.int32, (span, LANES), 1)
    for c in range(planes):
        parts = []
        for q in range(per):
            part = jnp.zeros((span, LANES), jnp.float32)
            for r in range(width):
                part = jnp.where(wide == r, values[r * per + q][c * span : (c + 1) * span], part)
            parts.append(part)
        sbuf[me, c * width : (c + 1) * width, :] = jnp.concatenate(parts, axis=0).T[:width]

    def exchange(p):
        return pltpu.make_async_remote_copy(
            src_ref=sbuf.at[me], dst_ref=sbuf.at[me], send_sem=ss_sem.at[p], recv_sem=sr_sem.at[me],
            device_id=device(p), device_id_type=MESH,
        )

    def arrived(p):
        return pltpu.make_async_remote_copy(
            src_ref=sbuf.at[p], dst_ref=sbuf.at[p], send_sem=ss_sem.at[p], recv_sem=sr_sem.at[p],
            device_id=device(p), device_id_type=MESH,
        )

    @pl.loop(1, n)
    def _(i):
        exchange(lax.rem(me + i, n)).start()

    @pl.loop(1, n)
    def _(i):
        arrived(lax.rem(me + n - i, n)).wait_recv()

    def plane(c, i):
        x = sbuf[:, c * width + i // per, :]
        q = i % per
        return x if q == 0 else pltpu.roll(x, LANES - q * span, 1)

    own_row = lax.broadcasted_iota(jnp.int32, (n, LANES), 0) == me
    one_row = lax.broadcasted_iota(jnp.int32, (1, LANES), 1)
    square = lax.broadcasted_iota(jnp.int32, (LANES, LANES), 0)
    loss_here = jnp.zeros((1, 1), jnp.float32)
    columns = []
    for c in range(planes):
        at = [(plane(c, b), plane(c, here + b)) for b in range(here)]
        token_loss, grad_at, mass, norm = loss_planes(at, *(plane(c, 2 * here + i) for i in range(4)))
        mine = one_row + c * span == me
        loss_here = loss_here + jnp.sum(
            jnp.where(mine & (one_row < span), token_loss, 0.0), axis=1, keepdims=True
        )
        lines = [norm, mass] + [jnp.sum(jnp.where(own_row, x, 0.0), axis=0, keepdims=True) for x in grad_at]
        stacked = jnp.zeros((LANES, LANES), jnp.float32)
        for i, line in enumerate(lines):
            stacked = jnp.where(square == i, line, stacked)
        columns.append(stacked.T[:span])
    loss_ref[...] = loss_here
    column = jnp.concatenate(columns, axis=0)
    norm, mass = column[:, 0:1], column[:, 1:2]
    logit_grad = -mass * jnp.exp(student - norm)
    added = [jnp.where(hits[b], column[:, 2 + b : 3 + b], 0.0) for b in range(here)]
    logit_grad = (logit_grad + jnp.concatenate(added, axis=1)).astype(jnp.bfloat16)

    step = 2 * LANES
    for j in range(0, ws.shape[0], step):
        product = lax.dot_general(
            logit_grad, ws[j : j + step, :], (((1,), (1,)), ((), ())), preferred_element_type=jnp.float32
        )
        for h in range(step // LANES):
            c = j // LANES + h
            ps[c * n : (c + 1) * n, :] = product[:, h * LANES : (h + 1) * LANES]

    def scatter(p):
        return pltpu.make_async_remote_copy(
            src_ref=pbuf.at[p], dst_ref=rbuf.at[me], send_sem=ps_sem.at[p], recv_sem=pr_sem.at[me],
            device_id=device(p), device_id_type=MESH,
        )

    def gathered(p):
        return pltpu.make_async_remote_copy(
            src_ref=pbuf.at[p], dst_ref=rbuf.at[p], send_sem=ps_sem.at[p], recv_sem=pr_sem.at[p],
            device_id=device(p), device_id_type=MESH,
        )

    @pl.loop(1, n)
    def _(i):
        p = lax.rem(me + i, n)
        pbuf[p] = ps[pl.ds(p, ds_rows, stride=n), :].astype(jnp.bfloat16)
        scatter(p).start()

    own = ps[pl.ds(me, ds_rows, stride=n), :].astype(jnp.bfloat16).astype(jnp.float32)

    def collect(i, total):
        p = lax.rem(me + n - i, n)
        gathered(p).wait_recv()
        return total + rbuf[p].astype(jnp.float32)

    total = lax.fori_loop(1, n, collect, own)
    grad_ref[...] = total.astype(jnp.bfloat16)

    @pl.loop(1, V)
    def _(d):
        to_z(d).wait_send()

    @pl.loop(0, V)
    def _(a):
        for d in range(1, T):
            to_xy(a, d).wait_send()
        for b in range(T):
            to_core(a, b).wait_send()

    @pl.loop(1, n)
    def _(i):
        p = lax.rem(me + i, n)
        exchange(p).wait_send()
        scatter(p).wait_send()


def local(sizes, student_hidden, teacher_hidden, student_head, teacher_head, proposed_block, proposed_offset):
    V, T, S = sizes
    n = V * T * S
    ds, width = student_head.shape
    dt = teacher_head.shape[0]
    ds_rows, dt_rows = ds // LANES, dt // LANES
    rows = ds_rows + dt_rows + 8
    K = proposed_block.shape[1]
    values = 2 * (width // BLK) + 4
    dma = pltpu.SemaphoreType.DMA
    loss, grad = pl.pallas_call(
        functools.partial(kernel, sizes),
        out_shape=(
            jax.ShapeDtypeStruct((1, 1), jnp.float32),
            jax.ShapeDtypeStruct((ds_rows, LANES), jnp.bfloat16),
        ),
        in_specs=[pl.BlockSpec(memory_space=pl.ANY)] * 6,
        out_specs=(pl.BlockSpec(memory_space=pltpu.VMEM), pl.BlockSpec(memory_space=pltpu.VMEM)),
        scratch_shapes=[
            pltpu.VMEM((1, ds), jnp.bfloat16),
            pltpu.VMEM((1, dt), jnp.bfloat16),
            pltpu.VMEM((ds, width), jnp.bfloat16),
            pltpu.VMEM((dt, width), jnp.bfloat16),
            pltpu.VMEM((1, K), jnp.int32),
            pltpu.VMEM((1, K), jnp.int32),
            pltpu.VMEM((rows, LANES), jnp.float32),
            pltpu.VMEM((n, rows, LANES), jnp.bfloat16),
            pltpu.VMEM((rows * n, LANES), jnp.float32),
            pltpu.VMEM((n, values * n // LANES, LANES), jnp.float32),
            pltpu.VMEM((ds_rows * n, LANES), jnp.float32),
            pltpu.VMEM((n, ds_rows, LANES), jnp.bfloat16),
            pltpu.VMEM((n, ds_rows, LANES), jnp.bfloat16),
            dma((6,)),
            dma((V,)),
            dma((V, T)),
            dma((V, T)),
            dma((n,)),
            dma((n,)),
            dma((n,)),
            dma((n,)),
            dma((n,)),
        ],
        compiler_params=pltpu.CompilerParams(
            collective_id=0, has_side_effects=True, vmem_limit_bytes=48 * 1024 * 1024
        ),
        name="distill",
    )(student_hidden, teacher_hidden, student_head, teacher_head, proposed_block, proposed_offset)
    return loss.reshape((1,)), grad.reshape((1, ds))


def solution(mesh):
    row = P(("groups", "vocab", "tokens", "sub"), None)
    return jax.shard_map(
        functools.partial(local, tuple(mesh.shape[a] for a in AXES)),
        mesh=mesh,
        in_specs=(row, row, P(None, AXES), P(None, AXES), row, row),
        out_specs=(P(("groups", "vocab", "tokens", "sub")), row),
        check_vma=False,
    )
```

```python
import functools
import math

import jax
import jax.numpy as jnp
from jax import lax
from jax.experimental import pallas as pl
from jax.experimental.pallas import tpu as pltpu
from jax.sharding import PartitionSpec as P

BLK = 128
LANES = 128
NONE = -1e30
AXES = ("vocab", "tokens", "sub")
mix_weight = 0.1
loss_scale = 64.0
MESH = pl.DeviceIdType.MESH


def loss_planes(at, student_max, student_sum, teacher_max, teacher_sum):
    top = lambda x: jnp.max(x, axis=0, keepdims=True)
    add = lambda x: jnp.sum(x, axis=0, keepdims=True)
    peak = top(student_max)
    student_norm = peak + jnp.log(add(student_sum * jnp.exp(student_max - peak)))
    teacher_peak = top(teacher_max)
    teacher_norm = teacher_peak + jnp.log(add(teacher_sum * jnp.exp(teacher_max - teacher_peak)))
    at_peak = functools.reduce(jnp.maximum, [top(s) for s, _ in at])
    shifted = [jnp.exp(s - at_peak) for s, _ in at]
    scale = 1.0 / sum(add(x) for x in shifted)
    weights = [x * scale for x in shifted]
    excess, direct = [], []
    for (student, teacher), weight in zip(at, weights):
        a = student - student_norm + math.log(mix_weight)
        b = teacher - teacher_norm + math.log(1.0 - mix_weight)
        mixture = jnp.maximum(a, b) + jnp.log(1.0 + jnp.exp(-jnp.abs(a - b)))
        excess.append(student - student_norm - mixture)
        direct.append(weight * (1.0 - jnp.exp(a - mixture)))
    token_loss = sum(add(w * e) for w, e in zip(weights, excess))
    grad_at = [loss_scale * (w * (e - token_loss) + d) for w, e, d in zip(weights, excess, direct)]
    mass = loss_scale * sum(add(d) for d in direct)
    return token_loss, grad_at, mass, student_norm


def kernel(
    sizes, sh_hbm, th_hbm, ws_hbm, wt_hbm, blk_hbm, off_hbm, loss_ref, grad_ref,
    sh, th, ws, wt, blk, off, stage, gbuf, xs, sbuf, ps, pbuf, rbuf,
    load_sem, gz_sem, gx_sem, gc_sem, gr_sem, ss_sem, sr_sem, ps_sem, pr_sem,
):
    V, T, S = sizes
    n = V * T * S
    g = lax.axis_index("groups")
    v, t, s = (lax.axis_index(a) for a in AXES)
    me = (v * T + t) * S + s
    ds_rows, dt_rows = sh.shape[1] // LANES, th.shape[1] // LANES
    rows = gbuf.shape[1]

    def slot(a, b, c):
        return (a * T + b) * S + c

    loads = [
        pltpu.make_async_copy(src, dst, load_sem.at[i])
        for i, (src, dst) in enumerate(
            [(sh_hbm, sh), (th_hbm, th), (blk_hbm, blk), (off_hbm, off), (ws_hbm, ws), (wt_hbm, wt)]
        )
    ]
    for load in loads:
        load.start()

    def turn(x, size):
        return jnp.where(x >= size, x - size, x)

    barrier = pltpu.get_barrier_semaphore()
    other = turn(s + 1, S)
    along = [turn(t + d, T) for d in range(T)]

    def greet(to):
        pl.semaphore_signal(barrier, inc=1, device_id=to, device_id_type=MESH)

    @pl.loop(1, V)
    def _(d):
        greet((g, turn(v + d, V), t, s))

    for d in range(1, T):
        greet((g, v, along[d], s))
    greet((g, v, t, other))

    for load in loads[:4]:
        load.wait()

    for j in range(ds_rows):
        stage[j : j + 1, :] = sh[:, j * LANES : (j + 1) * LANES].astype(jnp.float32)
    for j in range(dt_rows):
        stage[ds_rows + j : ds_rows + j + 1, :] = th[:, j * LANES : (j + 1) * LANES].astype(jnp.float32)
    K = blk.shape[1]
    base = ds_rows + dt_rows
    stage[base : base + 8, :] = jnp.zeros((8, LANES), jnp.float32)
    block_row = blk[...]
    stage[base : base + 1, :K] = (block_row // 64).astype(jnp.float32)
    stage[base + 1 : base + 2, :K] = (block_row % 64).astype(jnp.float32)
    stage[base + 2 : base + 3, :K] = off[...].astype(jnp.float32)
    gbuf[me] = stage[...].astype(jnp.bfloat16)

    pl.semaphore_wait(barrier, V - 1 + T - 1 + 1)

    def send(at, to, sem):
        return pltpu.make_async_remote_copy(
            src_ref=gbuf.at[at], dst_ref=gbuf.at[at], send_sem=sem, recv_sem=gr_sem.at[at],
            device_id=to, device_id_type=MESH,
        )

    def to_z(d):
        return send(me, (g, turn(v + d, V), t, s), gz_sem.at[d])

    def to_xy(a, d):
        return send(slot(a, t, s), (g, v, along[d], s), gx_sem.at[a, d])

    def to_core(a, b):
        return send(slot(a, b, s), (g, v, t, other), gc_sem.at[a, b])

    def unpack(at):
        xs[pl.ds(at, rows, stride=n), :] = gbuf[at].astype(jnp.float32)

    @pl.loop(1, V)
    def _(d):
        to_z(d).start()

    for d in range(1, T):
        to_xy(v, d).start()
    to_core(v, t).start()
    unpack(me)

    @pl.loop(1, V)
    def _(d):
        a = turn(v + V - d, V)
        send(slot(a, t, s), (g, v, t, other), gc_sem.at[a, t]).wait_recv()
        for e in range(1, T):
            to_xy(a, e).start()
        to_core(a, t).start()
        unpack(slot(a, t, s))

    @pl.loop(0, V)
    def _(d):
        a = turn(v + V - d, V)
        for e in range(1, T):
            b = along[(T - e) % T]
            to_core(a, b).wait_recv()
            to_core(a, b).start()
            unpack(slot(a, b, s))

    @pl.loop(0, V)
    def _(d):
        a = turn(v + V - d, V)
        for e in range(T):
            b = along[(T - e) % T]
            at = slot(a, b, other)
            send(at, (g, v, t, other), gc_sem.at[a, b]).wait_recv()
            unpack(at)

    def chunks(lo, hi):
        return jnp.concatenate([xs[c * n : (c + 1) * n, :] for c in range(lo, hi)], axis=1).astype(jnp.bfloat16)

    loads[4].wait()
    student = jnp.dot(chunks(0, ds_rows), ws[...], preferred_element_type=jnp.float32)
    loads[5].wait()
    teacher = jnp.dot(chunks(ds_rows, base), wt[...], preferred_element_type=jnp.float32)

    col_width = ws.shape[1]
    here = col_width // BLK
    block_all = xs[base * n : (base + 1) * n, :] * 64.0 + xs[(base + 1) * n : (base + 2) * n, :]
    offset_all = xs[(base + 2) * n : (base + 3) * n, :] + 1.0
    lane = lax.broadcasted_iota(jnp.int32, (n, LANES), 1)
    student_at, teacher_at, hits, masked = [], [], [], []
    for b in range(here):
        wanted = (me * here + b).astype(jnp.float32)
        chosen = jnp.where((block_all == wanted) & (lane < K), offset_all, 0.0)
        offset = jnp.sum(chosen, axis=1, keepdims=True)
        named = offset > 0.0
        hit = lane.astype(jnp.float32) + 1.0 == offset
        part = slice(b * BLK, (b + 1) * BLK)
        at_s = jnp.sum(jnp.where(hit, student[:, part], 0.0), axis=1, keepdims=True)
        student_at.append(jnp.where(named, at_s, NONE))
        teacher_at.append(jnp.sum(jnp.where(hit, teacher[:, part], 0.0), axis=1, keepdims=True))
        hits.append(hit)
        masked.append(jnp.where(named, teacher[:, part], NONE))
    teacher_seen = jnp.concatenate(masked, axis=1)
    student_max = jnp.max(student, axis=1, keepdims=True)
    student_sum = jnp.sum(jnp.exp(student - student_max), axis=1, keepdims=True)
    teacher_max = jnp.max(teacher_seen, axis=1, keepdims=True)
    teacher_sum = jnp.sum(
        jnp.where(teacher_seen > 0.5 * NONE, jnp.exp(teacher_seen - teacher_max), 0.0), axis=1, keepdims=True
    )
    values = student_at + teacher_at + [student_max, student_sum, teacher_max, teacher_sum]

    span = min(n, LANES)
    per = LANES // span
    planes = n // span
    width = len(values) // per
    wide = lax.broadcasted_iota(jnp.int32, (span, LANES), 1)
    for c in range(planes):
        parts = []
        for q in range(per):
            part = jnp.zeros((span, LANES), jnp.float32)
            for r in range(width):
                part = jnp.where(wide == r, values[r * per + q][c * span : (c + 1) * span], part)
            parts.append(part)
        sbuf[me, c * width : (c + 1) * width, :] = jnp.concatenate(parts, axis=0).T[:width]

    def everyone(act):
        for d in range(1, T * S + 1):
            b, c = along[d // S % T], (other if d % S else s)

            @pl.loop(1 if d == T * S else 0, V)
            def _(e):
                a = turn(v + e, V)
                act((g, a, b, c), slot(a, b, c))

    def exchange(to):
        return pltpu.make_async_remote_copy(
            src_ref=sbuf.at[me], dst_ref=sbuf.at[me], send_sem=ss_sem, recv_sem=sr_sem,
            device_id=to, device_id_type=MESH,
        )

    def scatter(to, p):
        return pltpu.make_async_remote_copy(
            src_ref=pbuf.at[p], dst_ref=rbuf.at[me], send_sem=ps_sem, recv_sem=pr_sem,
            device_id=to, device_id_type=MESH,
        )

    def total_of(buf, send_sem, recv_sem):
        part = buf.at[pl.ds(0, n - 1)]
        return pltpu.make_async_remote_copy(
            src_ref=part, dst_ref=part, send_sem=send_sem, recv_sem=recv_sem,
            device_id=(g, v, t, other), device_id_type=MESH,
        )

    everyone(lambda to, p: exchange(to).start())
    total_of(sbuf, ss_sem, sr_sem).wait_recv()

    def plane(c, i):
        x = sbuf[:, c * width + i // per, :]
        q = i % per
        return x if q == 0 else pltpu.roll(x, LANES - q * span, 1)

    own_row = lax.broadcasted_iota(jnp.int32, (n, LANES), 0) == me
    one_row = lax.broadcasted_iota(jnp.int32, (1, LANES), 1)
    square = lax.broadcasted_iota(jnp.int32, (LANES, LANES), 0)
    loss_here = jnp.zeros((1, 1), jnp.float32)
    columns = []
    for c in range(planes):
        at = [(plane(c, b), plane(c, here + b)) for b in range(here)]
        token_loss, grad_at, mass, norm = loss_planes(at, *(plane(c, 2 * here + i) for i in range(4)))
        mine = one_row + c * span == me
        loss_here = loss_here + jnp.sum(
            jnp.where(mine & (one_row < span), token_loss, 0.0), axis=1, keepdims=True
        )
        lines = [norm, mass] + [jnp.sum(jnp.where(own_row, x, 0.0), axis=0, keepdims=True) for x in grad_at]
        stacked = jnp.zeros((LANES, LANES), jnp.float32)
        for i, line in enumerate(lines):
            stacked = jnp.where(square == i, line, stacked)
        columns.append(stacked.T[:span])
    loss_ref[...] = loss_here
    column = jnp.concatenate(columns, axis=0)
    norm, mass = column[:, 0:1], column[:, 1:2]
    logit_grad = -mass * jnp.exp(student - norm)
    added = [jnp.where(hits[b], column[:, 2 + b : 3 + b], 0.0) for b in range(here)]
    logit_grad = (logit_grad + jnp.concatenate(added, axis=1)).astype(jnp.bfloat16)

    step = 2 * LANES
    for j in range(0, ws.shape[0], step):
        product = lax.dot_general(
            logit_grad, ws[j : j + step, :], (((1,), (1,)), ((), ())), preferred_element_type=jnp.float32
        )
        for h in range(step // LANES):
            c = j // LANES + h
            ps[c * n : (c + 1) * n, :] = product[:, h * LANES : (h + 1) * LANES]

    def pack(to, p):
        pbuf[p] = ps[pl.ds(p, ds_rows, stride=n), :].astype(jnp.bfloat16)
        scatter(to, p).start()

    everyone(pack)
    rbuf[me] = ps[pl.ds(me, ds_rows, stride=n), :].astype(jnp.bfloat16)
    total_of(rbuf, ps_sem, pr_sem).wait_recv()

    def collect(p, total):
        return total + rbuf[p].astype(jnp.float32)

    grad_ref[...] = lax.fori_loop(
        0, n, collect, jnp.zeros(grad_ref.shape, jnp.float32), unroll=8
    ).astype(jnp.bfloat16)

    @pl.loop(1, V)
    def _(d):
        to_z(d).wait_send()

    @pl.loop(0, V)
    def _(a):
        for d in range(1, T):
            to_xy(a, d).wait_send()
        for b in range(T):
            to_core(a, b).wait_send()

    total_of(sbuf, ss_sem, sr_sem).wait_send()
    total_of(rbuf, ps_sem, pr_sem).wait_send()


def local(sizes, student_hidden, teacher_hidden, student_head, teacher_head, proposed_block, proposed_offset):
    V, T, S = sizes
    n = V * T * S
    ds, width = student_head.shape
    dt = teacher_head.shape[0]
    ds_rows, dt_rows = ds // LANES, dt // LANES
    rows = ds_rows + dt_rows + 8
    K = proposed_block.shape[1]
    values = 2 * (width // BLK) + 4
    dma = pltpu.SemaphoreType.DMA
    loss, grad = pl.pallas_call(
        functools.partial(kernel, sizes),
        out_shape=(
            jax.ShapeDtypeStruct((1, 1), jnp.float32),
            jax.ShapeDtypeStruct((ds_rows, LANES), jnp.bfloat16),
        ),
        in_specs=[pl.BlockSpec(memory_space=pltpu.HBM)] * 6,
        out_specs=(pl.BlockSpec(memory_space=pltpu.VMEM), pl.BlockSpec(memory_space=pltpu.VMEM)),
        scratch_shapes=[
            pltpu.VMEM((1, ds), jnp.bfloat16),
            pltpu.VMEM((1, dt), jnp.bfloat16),
            pltpu.VMEM((ds, width), jnp.bfloat16),
            pltpu.VMEM((dt, width), jnp.bfloat16),
            pltpu.VMEM((1, K), jnp.int32),
            pltpu.VMEM((1, K), jnp.int32),
            pltpu.VMEM((rows, LANES), jnp.float32),
            pltpu.VMEM((n, rows, LANES), jnp.bfloat16),
            pltpu.VMEM((rows * n, LANES), jnp.float32),
            pltpu.VMEM((n, values * n // LANES, LANES), jnp.float32),
            pltpu.VMEM((ds_rows * n, LANES), jnp.float32),
            pltpu.VMEM((n, ds_rows, LANES), jnp.bfloat16),
            pltpu.VMEM((n, ds_rows, LANES), jnp.bfloat16),
            dma((6,)),
            dma((V,)),
            dma((V, T)),
            dma((V, T)),
            dma((n,)),
            dma,
            dma,
            dma,
            dma,
        ],
        compiler_params=pltpu.CompilerParams(
            collective_id=0, has_side_effects=True, vmem_limit_bytes=56 * 1024 * 1024
        ),
        name="distill",
    )(student_hidden, teacher_hidden, student_head, teacher_head, proposed_block, proposed_offset)
    return loss.reshape((1,)), grad.reshape((1, ds))


def solution(mesh):
    row = P(("groups", "vocab", "tokens", "sub"), None)
    return jax.shard_map(
        functools.partial(local, tuple(mesh.shape[a] for a in AXES)),
        mesh=mesh,
        in_specs=(row, row, P(None, AXES), P(None, AXES), row, row),
        out_specs=(P(("groups", "vocab", "tokens", "sub")), row),
        check_vma=False,
    )
```

```python
import functools
import math

import jax
import jax.numpy as jnp
from jax import lax
from jax.experimental import pallas as pl
from jax.experimental.pallas import tpu as pltpu
from jax.sharding import PartitionSpec as P

BLK = 128
LANES = 128
NONE = -1e30
AXES = ("vocab", "tokens", "sub")
mix_weight = 0.1
loss_scale = 64.0
MESH = pl.DeviceIdType.MESH


def loss_planes(at, student_max, student_sum, teacher_max, teacher_sum):
    top = lambda x: jnp.max(x, axis=0, keepdims=True)
    add = lambda x: jnp.sum(x, axis=0, keepdims=True)
    peak = top(student_max)
    student_norm = peak + jnp.log(add(student_sum * jnp.exp(student_max - peak)))
    teacher_peak = top(teacher_max)
    teacher_norm = teacher_peak + jnp.log(add(teacher_sum * jnp.exp(teacher_max - teacher_peak)))
    at_peak = functools.reduce(jnp.maximum, [top(s) for s, _ in at])
    shifted = [jnp.exp(s - at_peak) for s, _ in at]
    scale = 1.0 / sum(add(x) for x in shifted)
    weights = [x * scale for x in shifted]
    excess, direct = [], []
    for (student, teacher), weight in zip(at, weights):
        a = student - student_norm + math.log(mix_weight)
        b = teacher - teacher_norm + math.log(1.0 - mix_weight)
        mixture = jnp.maximum(a, b) + jnp.log(1.0 + jnp.exp(-jnp.abs(a - b)))
        excess.append(student - student_norm - mixture)
        direct.append(weight * (1.0 - jnp.exp(a - mixture)))
    token_loss = sum(add(w * e) for w, e in zip(weights, excess))
    grad_at = [loss_scale * (w * (e - token_loss) + d) for w, e, d in zip(weights, excess, direct)]
    mass = loss_scale * sum(add(d) for d in direct)
    return token_loss, grad_at, mass, student_norm


def kernel(
    sizes, sh_hbm, th_hbm, ws_hbm, wt_hbm, blk_hbm, off_hbm, loss_ref, grad_ref,
    sh, th, ws, wt, blk, off, stage, gbuf, xs, sbuf, ps, pbuf, rbuf,
    load_sem, gz_sem, gx_sem, gc_sem, gr_sem, ss_sem, sr_sem, ps_sem, pr_sem,
):
    V, T, S = sizes
    n = V * T * S
    g = lax.axis_index("groups")
    v, t, s = (lax.axis_index(a) for a in AXES)
    me = (v * T + t) * S + s
    ds_rows, dt_rows = sh.shape[1] // LANES, th.shape[1] // LANES
    rows = gbuf.shape[1]

    def slot(a, b, c):
        return (a * T + b) * S + c

    loads = [
        pltpu.make_async_copy(src, dst, load_sem.at[i])
        for i, (src, dst) in enumerate(
            [(sh_hbm, sh), (th_hbm, th), (blk_hbm, blk), (off_hbm, off), (ws_hbm, ws), (wt_hbm, wt)]
        )
    ]
    for load in loads:
        load.start()

    def turn(x, size):
        return jnp.where(x >= size, x - size, x)

    def outward(act, inward=False):
        @pl.loop(1, V)
        def _(d):
            d = V - d if inward else d

            @pl.when(v >= d)
            def _():
                act(v - d)

            @pl.when(v + d < V)
            def _():
                act(v + d)

    def inward(act):
        outward(act, inward=True)

    barrier = pltpu.get_barrier_semaphore()
    other = turn(s + 1, S)
    along = [turn(t + d, T) for d in range(T)]

    def greet(to):
        pl.semaphore_signal(barrier, inc=1, device_id=to, device_id_type=MESH)

    inward(lambda a: greet((g, a, t, s)))
    for d in range(1, T):
        greet((g, v, along[d], s))
    greet((g, v, t, other))

    for load in loads[:4]:
        load.wait()

    for j in range(ds_rows):
        stage[j : j + 1, :] = sh[:, j * LANES : (j + 1) * LANES].astype(jnp.float32)
    for j in range(dt_rows):
        stage[ds_rows + j : ds_rows + j + 1, :] = th[:, j * LANES : (j + 1) * LANES].astype(jnp.float32)
    K = blk.shape[1]
    base = ds_rows + dt_rows
    stage[base : base + 8, :] = jnp.zeros((8, LANES), jnp.float32)
    block_row = blk[...]
    stage[base : base + 1, :K] = (block_row // 64).astype(jnp.float32)
    stage[base + 1 : base + 2, :K] = (block_row % 64).astype(jnp.float32)
    stage[base + 2 : base + 3, :K] = off[...].astype(jnp.float32)
    gbuf[me] = stage[...].astype(jnp.bfloat16)

    pl.semaphore_wait(barrier, V - 1 + T - 1 + 1)

    def send(at, to, sem):
        return pltpu.make_async_remote_copy(
            src_ref=gbuf.at[at], dst_ref=gbuf.at[at], send_sem=sem, recv_sem=gr_sem.at[at],
            device_id=to, device_id_type=MESH,
        )

    def to_z(a):
        return send(me, (g, a, t, s), gz_sem.at[a])

    def to_xy(a, d):
        return send(slot(a, t, s), (g, v, along[d], s), gx_sem.at[a, d])

    def to_core(a, b):
        return send(slot(a, b, s), (g, v, t, other), gc_sem.at[a, b])

    def unpack(at):
        xs[pl.ds(at, rows, stride=n), :] = gbuf[at].astype(jnp.float32)

    inward(lambda a: to_z(a).start())
    for d in range(1, T):
        to_xy(v, d).start()
    to_core(v, t).start()
    unpack(me)

    def from_z(a):
        to_core(a, t).wait_recv()
        for e in range(1, T):
            to_xy(a, e).start()
        to_core(a, t).start()
        unpack(slot(a, t, s))

    def from_xy(a):
        for b in along[1:]:
            to_core(a, b).wait_recv()
            to_core(a, b).start()
            unpack(slot(a, b, s))

    def from_core(a):
        for b in along:
            at = slot(a, b, other)
            send(at, (g, v, t, other), gc_sem.at[a, b]).wait_recv()
            unpack(at)

    outward(from_z)
    for act in (from_xy, from_core):
        act(v)
        outward(act)

    def chunks(lo, hi):
        return jnp.concatenate([xs[c * n : (c + 1) * n, :] for c in range(lo, hi)], axis=1).astype(jnp.bfloat16)

    loads[4].wait()
    student = jnp.dot(chunks(0, ds_rows), ws[...], preferred_element_type=jnp.float32)
    loads[5].wait()
    teacher = jnp.dot(chunks(ds_rows, base), wt[...], preferred_element_type=jnp.float32)

    col_width = ws.shape[1]
    here = col_width // BLK
    block_all = xs[base * n : (base + 1) * n, :] * 64.0 + xs[(base + 1) * n : (base + 2) * n, :]
    offset_all = xs[(base + 2) * n : (base + 3) * n, :] + 1.0
    lane = lax.broadcasted_iota(jnp.int32, (n, LANES), 1)
    student_at, teacher_at, hits, masked = [], [], [], []
    for b in range(here):
        wanted = (me * here + b).astype(jnp.float32)
        chosen = jnp.where((block_all == wanted) & (lane < K), offset_all, 0.0)
        offset = jnp.sum(chosen, axis=1, keepdims=True)
        named = offset > 0.0
        hit = lane.astype(jnp.float32) + 1.0 == offset
        part = slice(b * BLK, (b + 1) * BLK)
        at_s = jnp.sum(jnp.where(hit, student[:, part], 0.0), axis=1, keepdims=True)
        student_at.append(jnp.where(named, at_s, NONE))
        teacher_at.append(jnp.sum(jnp.where(hit, teacher[:, part], 0.0), axis=1, keepdims=True))
        hits.append(hit)
        masked.append(jnp.where(named, teacher[:, part], NONE))
    teacher_seen = jnp.concatenate(masked, axis=1)
    student_max = jnp.max(student, axis=1, keepdims=True)
    student_sum = jnp.sum(jnp.exp(student - student_max), axis=1, keepdims=True)
    teacher_max = jnp.max(teacher_seen, axis=1, keepdims=True)
    teacher_sum = jnp.sum(
        jnp.where(teacher_seen > 0.5 * NONE, jnp.exp(teacher_seen - teacher_max), 0.0), axis=1, keepdims=True
    )
    values = student_at + teacher_at + [student_max, student_sum, teacher_max, teacher_sum]

    span = min(n, LANES)
    per = LANES // span
    planes = n // span
    width = len(values) // per
    wide = lax.broadcasted_iota(jnp.int32, (span, LANES), 1)
    for c in range(planes):
        parts = []
        for q in range(per):
            part = jnp.zeros((span, LANES), jnp.float32)
            for r in range(width):
                part = jnp.where(wide == r, values[r * per + q][c * span : (c + 1) * span], part)
            parts.append(part)
        sbuf[me, c * width : (c + 1) * width, :] = jnp.concatenate(parts, axis=0).T[:width]

    def everyone(act):
        places = [(along[d], c) for d in range(T) for c in (s, other)]

        def shard(a):
            for b, c in places:
                act((g, a, b, c), slot(a, b, c))

        inward(shard)
        for b, c in places[1:]:
            act((g, v, b, c), slot(v, b, c))

    def exchange(to):
        return pltpu.make_async_remote_copy(
            src_ref=sbuf.at[me], dst_ref=sbuf.at[me], send_sem=ss_sem, recv_sem=sr_sem,
            device_id=to, device_id_type=MESH,
        )

    def scatter(to, p):
        return pltpu.make_async_remote_copy(
            src_ref=pbuf.at[p], dst_ref=rbuf.at[me], send_sem=ps_sem, recv_sem=pr_sem,
            device_id=to, device_id_type=MESH,
        )

    def total_of(buf, send_sem, recv_sem):
        part = buf.at[pl.ds(0, n - 1)]
        return pltpu.make_async_remote_copy(
            src_ref=part, dst_ref=part, send_sem=send_sem, recv_sem=recv_sem,
            device_id=(g, v, t, other), device_id_type=MESH,
        )

    everyone(lambda to, p: exchange(to).start())
    total_of(sbuf, ss_sem, sr_sem).wait_recv()

    def plane(c, i):
        x = sbuf[:, c * width + i // per, :]
        q = i % per
        return x if q == 0 else pltpu.roll(x, LANES - q * span, 1)

    own_row = lax.broadcasted_iota(jnp.int32, (n, LANES), 0) == me
    one_row = lax.broadcasted_iota(jnp.int32, (1, LANES), 1)
    square = lax.broadcasted_iota(jnp.int32, (LANES, LANES), 0)
    loss_here = jnp.zeros((1, 1), jnp.float32)
    columns = []
    for c in range(planes):
        at = [(plane(c, b), plane(c, here + b)) for b in range(here)]
        token_loss, grad_at, mass, norm = loss_planes(at, *(plane(c, 2 * here + i) for i in range(4)))
        mine = one_row + c * span == me
        loss_here = loss_here + jnp.sum(
            jnp.where(mine & (one_row < span), token_loss, 0.0), axis=1, keepdims=True
        )
        lines = [norm, mass] + [jnp.sum(jnp.where(own_row, x, 0.0), axis=0, keepdims=True) for x in grad_at]
        stacked = jnp.zeros((LANES, LANES), jnp.float32)
        for i, line in enumerate(lines):
            stacked = jnp.where(square == i, line, stacked)
        columns.append(stacked.T[:span])
    loss_ref[...] = loss_here
    column = jnp.concatenate(columns, axis=0)
    norm, mass = column[:, 0:1], column[:, 1:2]
    logit_grad = -mass * jnp.exp(student - norm)
    added = [jnp.where(hits[b], column[:, 2 + b : 3 + b], 0.0) for b in range(here)]
    logit_grad = (logit_grad + jnp.concatenate(added, axis=1)).astype(jnp.bfloat16)

    step = 2 * LANES
    for j in range(0, ws.shape[0], step):
        product = lax.dot_general(
            logit_grad, ws[j : j + step, :], (((1,), (1,)), ((), ())), preferred_element_type=jnp.float32
        )
        for h in range(step // LANES):
            c = j // LANES + h
            ps[c * n : (c + 1) * n, :] = product[:, h * LANES : (h + 1) * LANES]

    def pack(to, p):
        pbuf[p] = ps[pl.ds(p, ds_rows, stride=n), :].astype(jnp.bfloat16)
        scatter(to, p).start()

    everyone(pack)
    rbuf[me] = ps[pl.ds(me, ds_rows, stride=n), :].astype(jnp.bfloat16)
    total_of(rbuf, ps_sem, pr_sem).wait_recv()

    def collect(p, total):
        return total + rbuf[p].astype(jnp.float32)

    grad_ref[...] = lax.fori_loop(
        0, n, collect, jnp.zeros(grad_ref.shape, jnp.float32), unroll=8
    ).astype(jnp.bfloat16)

    outward(lambda a: to_z(a).wait_send())

    @pl.loop(0, V)
    def _(a):
        for d in range(1, T):
            to_xy(a, d).wait_send()
        for b in range(T):
            to_core(a, b).wait_send()

    total_of(sbuf, ss_sem, sr_sem).wait_send()
    total_of(rbuf, ps_sem, pr_sem).wait_send()


def local(sizes, student_hidden, teacher_hidden, student_head, teacher_head, proposed_block, proposed_offset):
    V, T, S = sizes
    n = V * T * S
    ds, width = student_head.shape
    dt = teacher_head.shape[0]
    ds_rows, dt_rows = ds // LANES, dt // LANES
    rows = ds_rows + dt_rows + 8
    K = proposed_block.shape[1]
    values = 2 * (width // BLK) + 4
    dma = pltpu.SemaphoreType.DMA
    loss, grad = pl.pallas_call(
        functools.partial(kernel, sizes),
        out_shape=(
            jax.ShapeDtypeStruct((1, 1), jnp.float32),
            jax.ShapeDtypeStruct((ds_rows, LANES), jnp.bfloat16),
        ),
        in_specs=[pl.BlockSpec(memory_space=pltpu.HBM)] * 6,
        out_specs=(pl.BlockSpec(memory_space=pltpu.VMEM), pl.BlockSpec(memory_space=pltpu.VMEM)),
        scratch_shapes=[
            pltpu.VMEM((1, ds), jnp.bfloat16),
            pltpu.VMEM((1, dt), jnp.bfloat16),
            pltpu.VMEM((ds, width), jnp.bfloat16),
            pltpu.VMEM((dt, width), jnp.bfloat16),
            pltpu.VMEM((1, K), jnp.int32),
            pltpu.VMEM((1, K), jnp.int32),
            pltpu.VMEM((rows, LANES), jnp.float32),
            pltpu.VMEM((n, rows, LANES), jnp.bfloat16),
            pltpu.VMEM((rows * n, LANES), jnp.float32),
            pltpu.VMEM((n, values * n // LANES, LANES), jnp.float32),
            pltpu.VMEM((ds_rows * n, LANES), jnp.float32),
            pltpu.VMEM((n, ds_rows, LANES), jnp.bfloat16),
            pltpu.VMEM((n, ds_rows, LANES), jnp.bfloat16),
            dma((6,)),
            dma((V,)),
            dma((V, T)),
            dma((V, T)),
            dma((n,)),
            dma,
            dma,
            dma,
            dma,
        ],
        compiler_params=pltpu.CompilerParams(
            collective_id=0, has_side_effects=True, vmem_limit_bytes=56 * 1024 * 1024
        ),
        name="distill",
    )(student_hidden, teacher_hidden, student_head, teacher_head, proposed_block, proposed_offset)
    return loss.reshape((1,)), grad.reshape((1, ds))


def solution(mesh):
    row = P(("groups", "vocab", "tokens", "sub"), None)
    return jax.shard_map(
        functools.partial(local, tuple(mesh.shape[a] for a in AXES)),
        mesh=mesh,
        in_specs=(row, row, P(None, AXES), P(None, AXES), row, row),
        out_specs=(P(("groups", "vocab", "tokens", "sub")), row),
        check_vma=False,
    )
```

```python
import functools
import math

import jax
import jax.numpy as jnp
from jax import lax
from jax.experimental import pallas as pl
from jax.experimental.pallas import tpu as pltpu
from jax.sharding import PartitionSpec as P

BLK = 128
LANES = 128
NONE = -1e30
AXES = ("vocab", "tokens", "sub")
mix_weight = 0.1
loss_scale = 64.0
MESH = pl.DeviceIdType.MESH


def loss_planes(at, student_max, student_sum, teacher_max, teacher_sum):
    top = lambda x: jnp.max(x, axis=0, keepdims=True)
    add = lambda x: jnp.sum(x, axis=0, keepdims=True)
    peak = top(student_max)
    student_norm = peak + jnp.log(add(student_sum * jnp.exp(student_max - peak)))
    teacher_peak = top(teacher_max)
    teacher_norm = teacher_peak + jnp.log(add(teacher_sum * jnp.exp(teacher_max - teacher_peak)))
    at_peak = functools.reduce(jnp.maximum, [top(s) for s, _ in at])
    shifted = [jnp.exp(s - at_peak) for s, _ in at]
    scale = 1.0 / sum(add(x) for x in shifted)
    weights = [x * scale for x in shifted]
    excess, direct = [], []
    for (student, teacher), weight in zip(at, weights):
        a = student - student_norm + math.log(mix_weight)
        b = teacher - teacher_norm + math.log(1.0 - mix_weight)
        mixture = jnp.maximum(a, b) + jnp.log(1.0 + jnp.exp(-jnp.abs(a - b)))
        excess.append(student - student_norm - mixture)
        direct.append(weight * (1.0 - jnp.exp(a - mixture)))
    token_loss = sum(add(w * e) for w, e in zip(weights, excess))
    grad_at = [loss_scale * (w * (e - token_loss) + d) for w, e, d in zip(weights, excess, direct)]
    mass = loss_scale * sum(add(d) for d in direct)
    return token_loss, grad_at, mass, student_norm


def kernel(
    sizes, sh_hbm, th_hbm, ws_hbm, wt_hbm, blk_hbm, off_hbm, out_ref,
    sh, th, ws, wt, blk, off, stage, gbuf, xs, sbuf, ps, pbuf, rbuf,
    load_sem, gz_sem, gx_sem, gc_sem, gr_sem, ss_sem, sr_sem, ps_sem, pr_sem,
):
    V, T, S = sizes
    n = V * T * S
    g = lax.axis_index("groups")
    v, t, s = (lax.axis_index(a) for a in AXES)
    me = (v * T + t) * S + s
    ds_rows, dt_rows = sh.shape[1] // LANES, th.shape[1] // LANES
    rows = gbuf.shape[1]

    def slot(a, b, c):
        return (a * T + b) * S + c

    loads = [
        pltpu.make_async_copy(src, dst, load_sem.at[i])
        for i, (src, dst) in enumerate(
            [(sh_hbm, sh), (th_hbm, th), (blk_hbm, blk), (off_hbm, off), (ws_hbm, ws), (wt_hbm, wt)]
        )
    ]
    for load in loads:
        load.start()

    def turn(x, size):
        return jnp.where(x >= size, x - size, x)

    def outward(act, inward=False):
        @pl.loop(1, V)
        def _(d):
            d = V - d if inward else d

            @pl.when(v >= d)
            def _():
                act(v - d)

            @pl.when(v + d < V)
            def _():
                act(v + d)

    def inward(act):
        outward(act, inward=True)

    barrier = pltpu.get_barrier_semaphore()
    other = turn(s + 1, S)
    along = [turn(t + d, T) for d in range(T)]

    def greet(to):
        pl.semaphore_signal(barrier, inc=1, device_id=to, device_id_type=MESH)

    inward(lambda a: greet((g, a, t, s)))
    for d in range(1, T):
        greet((g, v, along[d], s))
    greet((g, v, t, other))

    for load in loads[:4]:
        load.wait()

    for j in range(ds_rows):
        stage[j : j + 1, :] = sh[:, j * LANES : (j + 1) * LANES].astype(jnp.float32)
    for j in range(dt_rows):
        stage[ds_rows + j : ds_rows + j + 1, :] = th[:, j * LANES : (j + 1) * LANES].astype(jnp.float32)
    K = blk.shape[1]
    base = ds_rows + dt_rows
    stage[base : base + 8, :] = jnp.zeros((8, LANES), jnp.float32)
    block_row = blk[...]
    stage[base : base + 1, :K] = (block_row // 64).astype(jnp.float32)
    stage[base + 1 : base + 2, :K] = (block_row % 64).astype(jnp.float32)
    stage[base + 2 : base + 3, :K] = off[...].astype(jnp.float32)
    gbuf[me] = stage[...].astype(jnp.bfloat16)

    pl.semaphore_wait(barrier, V - 1 + T - 1 + 1)

    def send(at, to, sem):
        return pltpu.make_async_remote_copy(
            src_ref=gbuf.at[at], dst_ref=gbuf.at[at], send_sem=sem, recv_sem=gr_sem.at[at],
            device_id=to, device_id_type=MESH,
        )

    def to_z(a):
        return send(me, (g, a, t, s), gz_sem.at[a])

    def to_xy(a, d):
        return send(slot(a, t, s), (g, v, along[d], s), gx_sem.at[a, d])

    def to_core(a, b):
        return send(slot(a, b, s), (g, v, t, other), gc_sem.at[a, b])

    def unpack(at):
        xs[pl.ds(at, rows, stride=n), :] = gbuf[at].astype(jnp.float32)

    inward(lambda a: to_z(a).start())
    for d in range(1, T):
        to_xy(v, d).start()
    to_core(v, t).start()
    unpack(me)

    def from_z(a):
        to_core(a, t).wait_recv()
        for e in range(1, T):
            to_xy(a, e).start()
        to_core(a, t).start()
        unpack(slot(a, t, s))

    def from_xy(a):
        for b in along[1:]:
            to_core(a, b).wait_recv()
            to_core(a, b).start()
            unpack(slot(a, b, s))

    def from_core(a):
        for b in along:
            at = slot(a, b, other)
            send(at, (g, v, t, other), gc_sem.at[a, b]).wait_recv()
            unpack(at)

    outward(from_z)
    for act in (from_xy, from_core):
        act(v)
        outward(act)

    def chunks(lo, hi):
        return jnp.concatenate([xs[c * n : (c + 1) * n, :] for c in range(lo, hi)], axis=1).astype(jnp.bfloat16)

    loads[4].wait()
    student = jnp.dot(chunks(0, ds_rows), ws[...], preferred_element_type=jnp.float32)
    loads[5].wait()
    teacher = jnp.dot(chunks(ds_rows, base), wt[...], preferred_element_type=jnp.float32)

    col_width = ws.shape[1]
    here = col_width // BLK
    block_all = xs[base * n : (base + 1) * n, :] * 64.0 + xs[(base + 1) * n : (base + 2) * n, :]
    offset_all = xs[(base + 2) * n : (base + 3) * n, :] + 1.0
    lane = lax.broadcasted_iota(jnp.int32, (n, LANES), 1)
    student_at, teacher_at, hits, masked = [], [], [], []
    for b in range(here):
        wanted = (me * here + b).astype(jnp.float32)
        chosen = jnp.where((block_all == wanted) & (lane < K), offset_all, 0.0)
        offset = jnp.sum(chosen, axis=1, keepdims=True)
        named = offset > 0.0
        hit = lane.astype(jnp.float32) + 1.0 == offset
        part = slice(b * BLK, (b + 1) * BLK)
        at_s = jnp.sum(jnp.where(hit, student[:, part], 0.0), axis=1, keepdims=True)
        student_at.append(jnp.where(named, at_s, NONE))
        teacher_at.append(jnp.sum(jnp.where(hit, teacher[:, part], 0.0), axis=1, keepdims=True))
        hits.append(hit)
        masked.append(jnp.where(named, teacher[:, part], NONE))
    teacher_seen = jnp.concatenate(masked, axis=1)
    student_max = jnp.max(student, axis=1, keepdims=True)
    student_sum = jnp.sum(jnp.exp(student - student_max), axis=1, keepdims=True)
    teacher_max = jnp.max(teacher_seen, axis=1, keepdims=True)
    teacher_sum = jnp.sum(
        jnp.where(teacher_seen > 0.5 * NONE, jnp.exp(teacher_seen - teacher_max), 0.0), axis=1, keepdims=True
    )
    values = student_at + teacher_at + [student_max, student_sum, teacher_max, teacher_sum]

    span = min(n, LANES)
    per = LANES // span
    planes = n // span
    width = len(values) // per
    wide = lax.broadcasted_iota(jnp.int32, (span, LANES), 1)
    for c in range(planes):
        parts = []
        for q in range(per):
            part = jnp.zeros((span, LANES), jnp.float32)
            for r in range(width):
                part = jnp.where(wide == r, values[r * per + q][c * span : (c + 1) * span], part)
            parts.append(part)
        sbuf[me, c * width : (c + 1) * width, :] = jnp.concatenate(parts, axis=0).T[:width]

    def everyone(act):
        places = [(along[d], c) for d in range(T) for c in (s, other)]

        def shard(a):
            for b, c in places:
                act((g, a, b, c), slot(a, b, c))

        inward(shard)
        for b, c in places[1:]:
            act((g, v, b, c), slot(v, b, c))

    def exchange(to):
        return pltpu.make_async_remote_copy(
            src_ref=sbuf.at[me], dst_ref=sbuf.at[me], send_sem=ss_sem, recv_sem=sr_sem,
            device_id=to, device_id_type=MESH,
        )

    def scatter(to, p):
        return pltpu.make_async_remote_copy(
            src_ref=pbuf.at[p], dst_ref=rbuf.at[me], send_sem=ps_sem, recv_sem=pr_sem,
            device_id=to, device_id_type=MESH,
        )

    def total_of(buf, send_sem, recv_sem):
        part = buf.at[pl.ds(0, n - 1)]
        return pltpu.make_async_remote_copy(
            src_ref=part, dst_ref=part, send_sem=send_sem, recv_sem=recv_sem,
            device_id=(g, v, t, other), device_id_type=MESH,
        )

    everyone(lambda to, p: exchange(to).start())
    total_of(sbuf, ss_sem, sr_sem).wait_recv()

    def plane(c, i):
        x = sbuf[:, c * width + i // per, :]
        q = i % per
        return x if q == 0 else pltpu.roll(x, LANES - q * span, 1)

    own_row = lax.broadcasted_iota(jnp.int32, (n, LANES), 0) == me
    one_row = lax.broadcasted_iota(jnp.int32, (1, LANES), 1)
    square = lax.broadcasted_iota(jnp.int32, (LANES, LANES), 0)
    loss_here = jnp.zeros((1, 1), jnp.float32)
    columns = []
    for c in range(planes):
        at = [(plane(c, b), plane(c, here + b)) for b in range(here)]
        token_loss, grad_at, mass, norm = loss_planes(at, *(plane(c, 2 * here + i) for i in range(4)))
        mine = one_row + c * span == me
        loss_here = loss_here + jnp.sum(
            jnp.where(mine & (one_row < span), token_loss, 0.0), axis=1, keepdims=True
        )
        lines = [norm, mass] + [jnp.sum(jnp.where(own_row, x, 0.0), axis=0, keepdims=True) for x in grad_at]
        stacked = jnp.zeros((LANES, LANES), jnp.float32)
        for i, line in enumerate(lines):
            stacked = jnp.where(square == i, line, stacked)
        columns.append(stacked.T[:span])
    out_ref[ds_rows:, :] = jnp.broadcast_to(loss_here, (8, LANES))
    column = jnp.concatenate(columns, axis=0)
    norm, mass = column[:, 0:1], column[:, 1:2]
    logit_grad = -mass * jnp.exp(student - norm)
    added = [jnp.where(hits[b], column[:, 2 + b : 3 + b], 0.0) for b in range(here)]
    logit_grad = (logit_grad + jnp.concatenate(added, axis=1)).astype(jnp.bfloat16)

    step = 2 * LANES
    for j in range(0, ws.shape[0], step):
        product = lax.dot_general(
            logit_grad, ws[j : j + step, :], (((1,), (1,)), ((), ())), preferred_element_type=jnp.float32
        )
        for h in range(step // LANES):
            c = j // LANES + h
            ps[c * n : (c + 1) * n, :] = product[:, h * LANES : (h + 1) * LANES]

    def pack(to, p):
        pbuf[p] = ps[pl.ds(p, ds_rows, stride=n), :].astype(jnp.bfloat16)
        scatter(to, p).start()

    everyone(pack)
    rbuf[me] = ps[pl.ds(me, ds_rows, stride=n), :].astype(jnp.bfloat16)
    total_of(rbuf, ps_sem, pr_sem).wait_recv()

    def collect(p, total):
        return total + rbuf[p].astype(jnp.float32)

    out_ref[:ds_rows, :] = lax.fori_loop(
        0, n, collect, jnp.zeros((ds_rows, LANES), jnp.float32), unroll=8
    )

    outward(lambda a: to_z(a).wait_send())

    @pl.loop(0, V)
    def _(a):
        for d in range(1, T):
            to_xy(a, d).wait_send()
        for b in range(T):
            to_core(a, b).wait_send()

    total_of(sbuf, ss_sem, sr_sem).wait_send()
    total_of(rbuf, ps_sem, pr_sem).wait_send()


def finish(out_ref, loss_ref, grad_ref):
    ds_rows = out_ref.shape[0] - 8
    for j in range(ds_rows):
        grad_ref[:, j * LANES : (j + 1) * LANES] = out_ref[j : j + 1, :].astype(jnp.bfloat16)
    loss_ref[...] = out_ref[ds_rows : ds_rows + 1, 0:1]


def local(sizes, student_hidden, teacher_hidden, student_head, teacher_head, proposed_block, proposed_offset):
    V, T, S = sizes
    n = V * T * S
    ds, width = student_head.shape
    dt = teacher_head.shape[0]
    ds_rows, dt_rows = ds // LANES, dt // LANES
    rows = ds_rows + dt_rows + 8
    K = proposed_block.shape[1]
    values = 2 * (width // BLK) + 4
    dma = pltpu.SemaphoreType.DMA
    result = pl.pallas_call(
        functools.partial(kernel, sizes),
        out_shape=jax.ShapeDtypeStruct((ds_rows + 8, LANES), jnp.float32),
        in_specs=[pl.BlockSpec(memory_space=pl.ANY)] * 6,
        out_specs=pl.BlockSpec(memory_space=pltpu.VMEM),
        scratch_shapes=[
            pltpu.VMEM((1, ds), jnp.bfloat16),
            pltpu.VMEM((1, dt), jnp.bfloat16),
            pltpu.VMEM((ds, width), jnp.bfloat16),
            pltpu.VMEM((dt, width), jnp.bfloat16),
            pltpu.VMEM((1, K), jnp.int32),
            pltpu.VMEM((1, K), jnp.int32),
            pltpu.VMEM((rows, LANES), jnp.float32),
            pltpu.VMEM((n, rows, LANES), jnp.bfloat16),
            pltpu.VMEM((rows * n, LANES), jnp.float32),
            pltpu.VMEM((n, values * n // LANES, LANES), jnp.float32),
            pltpu.VMEM((ds_rows * n, LANES), jnp.float32),
            pltpu.VMEM((n, ds_rows, LANES), jnp.bfloat16),
            pltpu.VMEM((n, ds_rows, LANES), jnp.bfloat16),
            dma((6,)),
            dma((V,)),
            dma((V, T)),
            dma((V, T)),
            dma((n,)),
            dma,
            dma,
            dma,
            dma,
        ],
        compiler_params=pltpu.CompilerParams(
            collective_id=0, has_side_effects=True, vmem_limit_bytes=56 * 1024 * 1024
        ),
        name="distill",
    )(student_hidden, teacher_hidden, student_head, teacher_head, proposed_block, proposed_offset)
    loss, grad = pl.pallas_call(
        finish,
        out_shape=(jax.ShapeDtypeStruct((1, 1), jnp.float32), jax.ShapeDtypeStruct((1, ds), jnp.bfloat16)),
        in_specs=[pl.BlockSpec(memory_space=pltpu.VMEM)],
        out_specs=(pl.BlockSpec(memory_space=pltpu.VMEM), pl.BlockSpec(memory_space=pltpu.VMEM)),
        name="finish",
    )(result)
    return loss.reshape((1,)), grad


def solution(mesh):
    row = P(("groups", "vocab", "tokens", "sub"), None)
    return jax.shard_map(
        functools.partial(local, tuple(mesh.shape[a] for a in AXES)),
        mesh=mesh,
        in_specs=(row, row, P(None, AXES), P(None, AXES), row, row),
        out_specs=(P(("groups", "vocab", "tokens", "sub")), row),
        check_vma=False,
    )
```

```python
import functools
import math

import jax
import jax.numpy as jnp
from jax import lax
from jax.experimental import pallas as pl
from jax.experimental.pallas import tpu as pltpu
from jax.sharding import PartitionSpec as P

BLK = 128
LANES = 128
NONE = -1e30
AXES = ("vocab", "tokens", "sub")
mix_weight = 0.1
loss_scale = 64.0
MESH = pl.DeviceIdType.MESH


def loss_planes(at, student_max, student_sum, teacher_max, teacher_sum):
    top = lambda x: jnp.max(x, axis=0, keepdims=True)
    add = lambda x: jnp.sum(x, axis=0, keepdims=True)
    peak = top(student_max)
    student_norm = peak + jnp.log(add(student_sum * jnp.exp(student_max - peak)))
    teacher_peak = top(teacher_max)
    teacher_norm = teacher_peak + jnp.log(add(teacher_sum * jnp.exp(teacher_max - teacher_peak)))
    at_peak = functools.reduce(jnp.maximum, [top(s) for s, _ in at])
    shifted = [jnp.exp(s - at_peak) for s, _ in at]
    scale = 1.0 / sum(add(x) for x in shifted)
    weights = [x * scale for x in shifted]
    excess, direct = [], []
    for (student, teacher), weight in zip(at, weights):
        a = student - student_norm + math.log(mix_weight)
        b = teacher - teacher_norm + math.log(1.0 - mix_weight)
        mixture = jnp.maximum(a, b) + jnp.log(1.0 + jnp.exp(-jnp.abs(a - b)))
        excess.append(student - student_norm - mixture)
        direct.append(weight * (1.0 - jnp.exp(a - mixture)))
    token_loss = sum(add(w * e) for w, e in zip(weights, excess))
    grad_at = [loss_scale * (w * (e - token_loss) + d) for w, e, d in zip(weights, excess, direct)]
    mass = loss_scale * sum(add(d) for d in direct)
    return token_loss, grad_at, mass, student_norm


def kernel(
    sizes, sh_hbm, th_hbm, ws_hbm, wt_hbm, blk_hbm, off_hbm, out_ref,
    sh, th, ws, wt, blk, off, stage, gbuf, xs, sbuf, ps, pbuf, rbuf,
    load_sem, gz_sem, gx_sem, gc_sem, gr_sem, ss_sem, sr_sem, ps_sem, pr_sem, cs_sem, cr_sem,
):
    V, T, S = sizes
    n = V * T * S
    g = lax.axis_index("groups")
    v, t, s = (lax.axis_index(a) for a in AXES)
    me = (v * T + t) * S + s
    ds_rows, dt_rows = sh.shape[1] // LANES, th.shape[1] // LANES
    rows = gbuf.shape[1]

    def slot(a, b, c):
        return (a * T + b) * S + c

    loads = [
        pltpu.make_async_copy(src, dst, load_sem.at[i])
        for i, (src, dst) in enumerate(
            [(sh_hbm, sh), (th_hbm, th), (blk_hbm, blk), (off_hbm, off), (ws_hbm, ws), (wt_hbm, wt)]
        )
    ]
    for load in loads:
        load.start()

    def turn(x, size):
        return jnp.where(x >= size, x - size, x)

    def outward(act, inward=False):
        @pl.loop(1, V)
        def _(d):
            d = V - d if inward else d

            @pl.when(v >= d)
            def _():
                act(v - d)

            @pl.when(v + d < V)
            def _():
                act(v + d)

    def inward(act):
        outward(act, inward=True)

    barrier = pltpu.get_barrier_semaphore()
    other = turn(s + 1, S)
    along = [turn(t + d, T) for d in range(T)]

    def greet(to):
        pl.semaphore_signal(barrier, inc=1, device_id=to, device_id_type=MESH)

    inward(lambda a: greet((g, a, t, s)))
    for d in range(1, T):
        greet((g, v, along[d], s))
    greet((g, v, t, other))

    for load in loads[:4]:
        load.wait()

    for j in range(ds_rows):
        stage[j : j + 1, :] = sh[:, j * LANES : (j + 1) * LANES].astype(jnp.float32)
    for j in range(dt_rows):
        stage[ds_rows + j : ds_rows + j + 1, :] = th[:, j * LANES : (j + 1) * LANES].astype(jnp.float32)
    K = blk.shape[1]
    base = ds_rows + dt_rows
    stage[base : base + 8, :] = jnp.zeros((8, LANES), jnp.float32)
    block_row = blk[...]
    stage[base : base + 1, :K] = (block_row // 64).astype(jnp.float32)
    stage[base + 1 : base + 2, :K] = (block_row % 64).astype(jnp.float32)
    stage[base + 2 : base + 3, :K] = off[...].astype(jnp.float32)
    gbuf[me] = stage[...].astype(jnp.bfloat16)

    pl.semaphore_wait(barrier, V - 1 + T - 1 + 1)

    def send(at, to, sem):
        return pltpu.make_async_remote_copy(
            src_ref=gbuf.at[at], dst_ref=gbuf.at[at], send_sem=sem, recv_sem=gr_sem.at[at],
            device_id=to, device_id_type=MESH,
        )

    def to_z(a):
        return send(me, (g, a, t, s), gz_sem.at[a])

    def to_xy(a, d):
        return send(slot(a, t, s), (g, v, along[d], s), gx_sem.at[a, d])

    def to_core(a, b):
        return send(slot(a, b, s), (g, v, t, other), gc_sem.at[a, b])

    def unpack(at):
        xs[pl.ds(at, rows, stride=n), :] = gbuf[at].astype(jnp.float32)

    inward(lambda a: to_z(a).start())
    for d in range(1, T):
        to_xy(v, d).start()
    to_core(v, t).start()
    unpack(me)

    def from_z(a):
        to_core(a, t).wait_recv()
        for e in range(1, T):
            to_xy(a, e).start()
        to_core(a, t).start()
        unpack(slot(a, t, s))

    def from_xy(a):
        for b in along[1:]:
            to_core(a, b).wait_recv()
            to_core(a, b).start()
            unpack(slot(a, b, s))

    def from_core(a):
        for b in along:
            at = slot(a, b, other)
            send(at, (g, v, t, other), gc_sem.at[a, b]).wait_recv()
            unpack(at)

    outward(from_z)
    for act in (from_xy, from_core):
        act(v)
        outward(act)

    def chunks(lo, hi):
        return jnp.concatenate([xs[c * n : (c + 1) * n, :] for c in range(lo, hi)], axis=1).astype(jnp.bfloat16)

    loads[4].wait()
    student = jnp.dot(chunks(0, ds_rows), ws[...], preferred_element_type=jnp.float32)
    loads[5].wait()
    teacher = jnp.dot(chunks(ds_rows, base), wt[...], preferred_element_type=jnp.float32)

    col_width = ws.shape[1]
    here = col_width // BLK
    block_all = xs[base * n : (base + 1) * n, :] * 64.0 + xs[(base + 1) * n : (base + 2) * n, :]
    offset_all = xs[(base + 2) * n : (base + 3) * n, :] + 1.0
    lane = lax.broadcasted_iota(jnp.int32, (n, LANES), 1)
    student_at, teacher_at, hits, masked = [], [], [], []
    for b in range(here):
        wanted = (me * here + b).astype(jnp.float32)
        chosen = jnp.where((block_all == wanted) & (lane < K), offset_all, 0.0)
        offset = jnp.sum(chosen, axis=1, keepdims=True)
        named = offset > 0.0
        hit = lane.astype(jnp.float32) + 1.0 == offset
        part = slice(b * BLK, (b + 1) * BLK)
        at_s = jnp.sum(jnp.where(hit, student[:, part], 0.0), axis=1, keepdims=True)
        student_at.append(jnp.where(named, at_s, NONE))
        teacher_at.append(jnp.sum(jnp.where(hit, teacher[:, part], 0.0), axis=1, keepdims=True))
        hits.append(hit)
        masked.append(jnp.where(named, teacher[:, part], NONE))
    teacher_seen = jnp.concatenate(masked, axis=1)
    student_max = jnp.max(student, axis=1, keepdims=True)
    student_sum = jnp.sum(jnp.exp(student - student_max), axis=1, keepdims=True)
    teacher_max = jnp.max(teacher_seen, axis=1, keepdims=True)
    teacher_sum = jnp.sum(
        jnp.where(teacher_seen > 0.5 * NONE, jnp.exp(teacher_seen - teacher_max), 0.0), axis=1, keepdims=True
    )
    values = student_at + teacher_at + [student_max, student_sum, teacher_max, teacher_sum]

    span = min(n, LANES)
    per = LANES // span
    planes = n // span
    width = len(values) // per
    wide = lax.broadcasted_iota(jnp.int32, (span, LANES), 1)
    for c in range(planes):
        parts = []
        for q in range(per):
            part = jnp.zeros((span, LANES), jnp.float32)
            for r in range(width):
                part = jnp.where(wide == r, values[r * per + q][c * span : (c + 1) * span], part)
            parts.append(part)
        sbuf[me, c * width : (c + 1) * width, :] = jnp.concatenate(parts, axis=0).T[:width]

    def everyone(act):
        places = [(along[d], c) for d in range(T) for c in (s, other)]

        def shard(a):
            for b, c in places:
                act((g, a, b, c), slot(a, b, c))

        inward(shard)
        for b, c in places[1:]:
            act((g, v, b, c), slot(v, b, c))

    def exchange(to):
        return pltpu.make_async_remote_copy(
            src_ref=sbuf.at[me], dst_ref=sbuf.at[me], send_sem=ss_sem, recv_sem=sr_sem,
            device_id=to, device_id_type=MESH,
        )

    chips = V * T

    def to_pair(a):
        return pltpu.make_async_remote_copy(
            src_ref=pbuf.at[pl.ds(a * T, T)], dst_ref=rbuf.at[pl.ds(a * T, T)],
            send_sem=cs_sem.at[a], recv_sem=cr_sem.at[a],
            device_id=(g, v, t, other), device_id_type=MESH,
        )

    def scatter(a, b):
        return pltpu.make_async_remote_copy(
            src_ref=pbuf.at[chips + a * T + b], dst_ref=rbuf.at[chips + v * T + t], send_sem=ps_sem, recv_sem=pr_sem,
            device_id=(g, a, b, s), device_id_type=MESH,
        )

    def total_of(buf, count, send_sem, recv_sem):
        part = buf.at[pl.ds(0, count)]
        return pltpu.make_async_remote_copy(
            src_ref=part, dst_ref=part, send_sem=send_sem, recv_sem=recv_sem,
            device_id=(g, v, t, other), device_id_type=MESH,
        )

    everyone(lambda to, p: exchange(to).start())
    total_of(sbuf, n - 1, ss_sem, sr_sem).wait_recv()

    def plane(c, i):
        x = sbuf[:, c * width + i // per, :]
        q = i % per
        return x if q == 0 else pltpu.roll(x, LANES - q * span, 1)

    own_row = lax.broadcasted_iota(jnp.int32, (n, LANES), 0) == me
    one_row = lax.broadcasted_iota(jnp.int32, (1, LANES), 1)
    square = lax.broadcasted_iota(jnp.int32, (LANES, LANES), 0)
    loss_here = jnp.zeros((1, 1), jnp.float32)
    columns = []
    for c in range(planes):
        at = [(plane(c, b), plane(c, here + b)) for b in range(here)]
        token_loss, grad_at, mass, norm = loss_planes(at, *(plane(c, 2 * here + i) for i in range(4)))
        mine = one_row + c * span == me
        loss_here = loss_here + jnp.sum(
            jnp.where(mine & (one_row < span), token_loss, 0.0), axis=1, keepdims=True
        )
        lines = [norm, mass] + [jnp.sum(jnp.where(own_row, x, 0.0), axis=0, keepdims=True) for x in grad_at]
        stacked = jnp.zeros((LANES, LANES), jnp.float32)
        for i, line in enumerate(lines):
            stacked = jnp.where(square == i, line, stacked)
        columns.append(stacked.T[:span])
    out_ref[ds_rows:, :] = jnp.broadcast_to(loss_here, (8, LANES))
    column = jnp.concatenate(columns, axis=0)
    norm, mass = column[:, 0:1], column[:, 1:2]
    logit_grad = -mass * jnp.exp(student - norm)
    added = [jnp.where(hits[b], column[:, 2 + b : 3 + b], 0.0) for b in range(here)]
    logit_grad = (logit_grad + jnp.concatenate(added, axis=1)).astype(jnp.bfloat16)

    step = 2 * LANES
    for j in range(0, ws.shape[0], step):
        product = lax.dot_general(
            logit_grad, ws[j : j + step, :], (((1,), (1,)), ((), ())), preferred_element_type=jnp.float32
        )
        for h in range(step // LANES):
            c = j // LANES + h
            ps[c * n : (c + 1) * n, :] = product[:, h * LANES : (h + 1) * LANES]

    def partial(p):
        return ps[pl.ds(p, ds_rows, stride=n), :].astype(jnp.bfloat16)

    def give(a):
        for b in range(T):
            pbuf[a * T + b] = partial(slot(a, b, other))
        to_pair(a).start()

    inward(give)
    give(v)

    def paired(a, b):
        return (partial(slot(a, b, s)).astype(jnp.float32) + rbuf[a * T + b].astype(jnp.float32)).astype(jnp.bfloat16)

    def pack(a):
        to_pair(a).wait_recv()
        for b in along:
            pbuf[chips + a * T + b] = paired(a, b)
            scatter(a, b).start()

    inward(pack)
    to_pair(v).wait_recv()
    for b in along[1:]:
        pbuf[chips + v * T + b] = paired(v, b)
        scatter(v, b).start()
    rbuf[chips + v * T + t] = paired(v, t)
    total_of(rbuf, chips - 1, ps_sem, pr_sem).wait_recv()

    def collect(q, total):
        return total + rbuf[chips + q].astype(jnp.float32)

    out_ref[:ds_rows, :] = lax.fori_loop(
        0, chips, collect, jnp.zeros((ds_rows, LANES), jnp.float32), unroll=8
    )

    outward(lambda a: to_z(a).wait_send())

    @pl.loop(0, V)
    def _(a):
        for d in range(1, T):
            to_xy(a, d).wait_send()
        for b in range(T):
            to_core(a, b).wait_send()

    total_of(sbuf, n - 1, ss_sem, sr_sem).wait_send()

    @pl.loop(0, V)
    def _(a):
        to_pair(a).wait_send()

    total_of(rbuf, chips - 1, ps_sem, pr_sem).wait_send()


def finish(out_ref, loss_ref, grad_ref):
    ds_rows = out_ref.shape[0] - 8
    for j in range(ds_rows):
        grad_ref[:, j * LANES : (j + 1) * LANES] = out_ref[j : j + 1, :].astype(jnp.bfloat16)
    loss_ref[...] = out_ref[ds_rows : ds_rows + 1, 0:1]


def local(sizes, student_hidden, teacher_hidden, student_head, teacher_head, proposed_block, proposed_offset):
    V, T, S = sizes
    n = V * T * S
    ds, width = student_head.shape
    dt = teacher_head.shape[0]
    ds_rows, dt_rows = ds // LANES, dt // LANES
    rows = ds_rows + dt_rows + 8
    K = proposed_block.shape[1]
    values = 2 * (width // BLK) + 4
    dma = pltpu.SemaphoreType.DMA
    result = pl.pallas_call(
        functools.partial(kernel, sizes),
        out_shape=jax.ShapeDtypeStruct((ds_rows + 8, LANES), jnp.float32),
        in_specs=[pl.BlockSpec(memory_space=pl.ANY)] * 6,
        out_specs=pl.BlockSpec(memory_space=pltpu.VMEM),
        scratch_shapes=[
            pltpu.VMEM((1, ds), jnp.bfloat16),
            pltpu.VMEM((1, dt), jnp.bfloat16),
            pltpu.VMEM((ds, width), jnp.bfloat16),
            pltpu.VMEM((dt, width), jnp.bfloat16),
            pltpu.VMEM((1, K), jnp.int32),
            pltpu.VMEM((1, K), jnp.int32),
            pltpu.VMEM((rows, LANES), jnp.float32),
            pltpu.VMEM((n, rows, LANES), jnp.bfloat16),
            pltpu.VMEM((rows * n, LANES), jnp.float32),
            pltpu.VMEM((n, values * n // LANES, LANES), jnp.float32),
            pltpu.VMEM((ds_rows * n, LANES), jnp.float32),
            pltpu.VMEM((n, ds_rows, LANES), jnp.bfloat16),
            pltpu.VMEM((n, ds_rows, LANES), jnp.bfloat16),
            dma((6,)),
            dma((V,)),
            dma((V, T)),
            dma((V, T)),
            dma((n,)),
            dma,
            dma,
            dma,
            dma,
            dma((V,)),
            dma((V,)),
        ],
        compiler_params=pltpu.CompilerParams(
            collective_id=0, has_side_effects=True, vmem_limit_bytes=56 * 1024 * 1024
        ),
        name="distill",
    )(student_hidden, teacher_hidden, student_head, teacher_head, proposed_block, proposed_offset)
    loss, grad = pl.pallas_call(
        finish,
        out_shape=(jax.ShapeDtypeStruct((1, 1), jnp.float32), jax.ShapeDtypeStruct((1, ds), jnp.bfloat16)),
        in_specs=[pl.BlockSpec(memory_space=pltpu.VMEM)],
        out_specs=(pl.BlockSpec(memory_space=pltpu.VMEM), pl.BlockSpec(memory_space=pltpu.VMEM)),
        compiler_params=pltpu.CompilerParams(vmem_limit_bytes=56 * 1024 * 1024),
        name="finish",
    )(result)
    return loss.reshape((1,)), grad


def solution(mesh):
    row = P(("groups", "vocab", "tokens", "sub"), None)
    return jax.shard_map(
        functools.partial(local, tuple(mesh.shape[a] for a in AXES)),
        mesh=mesh,
        in_specs=(row, row, P(None, AXES), P(None, AXES), row, row),
        out_specs=(P(("groups", "vocab", "tokens", "sub")), row),
        check_vma=False,
    )
```

```python
import functools
import math

import jax
import jax.numpy as jnp
from jax import lax
from jax.experimental import pallas as pl
from jax.experimental.pallas import tpu as pltpu
from jax.sharding import PartitionSpec as P

BLK = 128
LANES = 128
NONE = -1e30
AXES = ("vocab", "tokens", "sub")
mix_weight = 0.1
loss_scale = 64.0
MESH = pl.DeviceIdType.MESH


def loss_planes(at, student_max, student_sum, teacher_max, teacher_sum):
    top = lambda x: jnp.max(x, axis=0, keepdims=True)
    add = lambda x: jnp.sum(x, axis=0, keepdims=True)
    peak = top(student_max)
    student_norm = peak + jnp.log(add(student_sum * jnp.exp(student_max - peak)))
    teacher_peak = top(teacher_max)
    teacher_norm = teacher_peak + jnp.log(add(teacher_sum * jnp.exp(teacher_max - teacher_peak)))
    at_peak = functools.reduce(jnp.maximum, [top(s) for s, _ in at])
    shifted = [jnp.exp(s - at_peak) for s, _ in at]
    scale = 1.0 / sum(add(x) for x in shifted)
    weights = [x * scale for x in shifted]
    excess, direct = [], []
    for (student, teacher), weight in zip(at, weights):
        a = student - student_norm + math.log(mix_weight)
        b = teacher - teacher_norm + math.log(1.0 - mix_weight)
        mixture = jnp.maximum(a, b) + jnp.log(1.0 + jnp.exp(-jnp.abs(a - b)))
        excess.append(student - student_norm - mixture)
        direct.append(weight * (1.0 - jnp.exp(a - mixture)))
    token_loss = sum(add(w * e) for w, e in zip(weights, excess))
    grad_at = [loss_scale * (w * (e - token_loss) + d) for w, e, d in zip(weights, excess, direct)]
    mass = loss_scale * sum(add(d) for d in direct)
    return token_loss, grad_at, mass, student_norm


def kernel(
    sizes, sh_hbm, th_hbm, ws_hbm, wt_hbm, blk_hbm, off_hbm, out_ref,
    sh, th, ws, wt, blk, off, stage, gbuf, xs, sbuf, ps, pbuf, rbuf,
    load_sem, gz_sem, gx_sem, gc_sem, gr_sem, ss_sem, sr_sem, ps_sem, pr_sem, cs_sem, cr_sem,
):
    V, T, S = sizes
    n = V * T * S
    g = lax.axis_index("groups")
    v, t, s = (lax.axis_index(a) for a in AXES)
    me = (v * T + t) * S + s
    ds_rows, dt_rows = sh.shape[1] // LANES, th.shape[1] // LANES
    rows = gbuf.shape[1]

    def slot(a, b, c):
        return (a * T + b) * S + c

    loads = [
        pltpu.make_async_copy(src, dst, load_sem.at[i])
        for i, (src, dst) in enumerate(
            [(sh_hbm, sh), (th_hbm, th), (blk_hbm, blk), (off_hbm, off), (ws_hbm, ws), (wt_hbm, wt)]
        )
    ]
    for load in loads:
        load.start()

    def turn(x, size):
        return jnp.where(x >= size, x - size, x)

    def outward(act, inward=False):
        @pl.loop(1, V)
        def _(d):
            d = V - d if inward else d

            @pl.when(v >= d)
            def _():
                act(v - d)

            @pl.when(v + d < V)
            def _():
                act(v + d)

    def inward(act):
        outward(act, inward=True)

    barrier = pltpu.get_barrier_semaphore()
    other = turn(s + 1, S)
    along = [turn(t + d, T) for d in range(T)]

    def greet(to):
        pl.semaphore_signal(barrier, inc=1, device_id=to, device_id_type=MESH)

    inward(lambda a: greet((g, a, t, s)))
    for d in range(1, T):
        greet((g, v, along[d], s))
    greet((g, v, t, other))

    for load in loads[:4]:
        load.wait()

    for j in range(ds_rows):
        stage[j : j + 1, :] = sh[:, j * LANES : (j + 1) * LANES].astype(jnp.float32)
    for j in range(dt_rows):
        stage[ds_rows + j : ds_rows + j + 1, :] = th[:, j * LANES : (j + 1) * LANES].astype(jnp.float32)
    K = blk.shape[1]
    base = ds_rows + dt_rows
    stage[base : base + 8, :] = jnp.zeros((8, LANES), jnp.float32)
    block_row = blk[...]
    stage[base : base + 1, :K] = (block_row // 64).astype(jnp.float32)
    stage[base + 1 : base + 2, :K] = (block_row % 64).astype(jnp.float32)
    stage[base + 2 : base + 3, :K] = off[...].astype(jnp.float32)
    gbuf[me] = stage[...].astype(jnp.bfloat16)

    pl.semaphore_wait(barrier, V - 1 + T - 1 + 1)

    def send(at, to, sem):
        return pltpu.make_async_remote_copy(
            src_ref=gbuf.at[at], dst_ref=gbuf.at[at], send_sem=sem, recv_sem=gr_sem.at[at],
            device_id=to, device_id_type=MESH,
        )

    def to_z(a):
        return send(me, (g, a, t, s), gz_sem.at[a])

    def to_xy(a, d):
        return send(slot(a, t, s), (g, v, along[d], s), gx_sem.at[a, d])

    def to_core(a, b):
        return send(slot(a, b, s), (g, v, t, other), gc_sem.at[a, b])

    def unpack(at):
        xs[pl.ds(at, rows, stride=n), :] = gbuf[at].astype(jnp.float32)

    inward(lambda a: to_z(a).start())
    for d in range(1, T):
        to_xy(v, d).start()
    to_core(v, t).start()
    unpack(me)

    def from_z(a):
        to_core(a, t).wait_recv()
        for e in range(1, T):
            to_xy(a, e).start()
        to_core(a, t).start()
        unpack(slot(a, t, s))

    def from_xy(a):
        for b in along[1:]:
            to_core(a, b).wait_recv()
            to_core(a, b).start()
            unpack(slot(a, b, s))

    def from_core(a):
        for b in along:
            at = slot(a, b, other)
            send(at, (g, v, t, other), gc_sem.at[a, b]).wait_recv()
            unpack(at)

    outward(from_z)
    for act in (from_xy, from_core):
        act(v)
        outward(act)

    def chunks(lo, hi):
        return jnp.concatenate([xs[c * n : (c + 1) * n, :] for c in range(lo, hi)], axis=1).astype(jnp.bfloat16)

    loads[4].wait()
    student = jnp.dot(chunks(0, ds_rows), ws[...], preferred_element_type=jnp.float32)
    loads[5].wait()
    teacher = jnp.dot(chunks(ds_rows, base), wt[...], preferred_element_type=jnp.float32)

    col_width = ws.shape[1]
    here = col_width // BLK
    block_all = xs[base * n : (base + 1) * n, :] * 64.0 + xs[(base + 1) * n : (base + 2) * n, :]
    offset_all = xs[(base + 2) * n : (base + 3) * n, :] + 1.0
    lane = lax.broadcasted_iota(jnp.int32, (n, LANES), 1)
    student_at, teacher_at, hits, masked = [], [], [], []
    for b in range(here):
        wanted = (me * here + b).astype(jnp.float32)
        chosen = jnp.where((block_all == wanted) & (lane < K), offset_all, 0.0)
        offset = jnp.sum(chosen, axis=1, keepdims=True)
        named = offset > 0.0
        hit = lane.astype(jnp.float32) + 1.0 == offset
        part = slice(b * BLK, (b + 1) * BLK)
        at_s = jnp.sum(jnp.where(hit, student[:, part], 0.0), axis=1, keepdims=True)
        student_at.append(jnp.where(named, at_s, NONE))
        teacher_at.append(jnp.sum(jnp.where(hit, teacher[:, part], 0.0), axis=1, keepdims=True))
        hits.append(hit)
        masked.append(jnp.where(named, teacher[:, part], NONE))
    teacher_seen = jnp.concatenate(masked, axis=1)
    student_max = jnp.max(student, axis=1, keepdims=True)
    student_sum = jnp.sum(jnp.exp(student - student_max), axis=1, keepdims=True)
    teacher_max = jnp.max(teacher_seen, axis=1, keepdims=True)
    teacher_sum = jnp.sum(
        jnp.where(teacher_seen > 0.5 * NONE, jnp.exp(teacher_seen - teacher_max), 0.0), axis=1, keepdims=True
    )
    values = student_at + teacher_at + [student_max, student_sum, teacher_max, teacher_sum]

    span = min(n, LANES)
    per = LANES // span
    planes = n // span
    width = len(values) // per
    wide = lax.broadcasted_iota(jnp.int32, (span, LANES), 1)
    for c in range(planes):
        parts = []
        for q in range(per):
            part = jnp.zeros((span, LANES), jnp.float32)
            for r in range(width):
                part = jnp.where(wide == r, values[r * per + q][c * span : (c + 1) * span], part)
            parts.append(part)
        sbuf[me, c * width : (c + 1) * width, :] = jnp.concatenate(parts, axis=0).T[:width]

    def everyone(act):
        places = [(along[d], c) for d in range(T) for c in (s, other)]

        def shard(a):
            for b, c in places:
                act((g, a, b, c), slot(a, b, c))

        inward(shard)
        for b, c in places[1:]:
            act((g, v, b, c), slot(v, b, c))

    def exchange(to):
        return pltpu.make_async_remote_copy(
            src_ref=sbuf.at[me], dst_ref=sbuf.at[me], send_sem=ss_sem, recv_sem=sr_sem,
            device_id=to, device_id_type=MESH,
        )

    chips = V * T

    def to_pair(a):
        return pltpu.make_async_remote_copy(
            src_ref=pbuf.at[pl.ds(a * T, T)], dst_ref=rbuf.at[pl.ds(a * T, T)],
            send_sem=cs_sem.at[a], recv_sem=cr_sem.at[a],
            device_id=(g, v, t, other), device_id_type=MESH,
        )

    def scatter(a, b):
        return pltpu.make_async_remote_copy(
            src_ref=pbuf.at[chips + a * T + b], dst_ref=rbuf.at[chips + v * T + t], send_sem=ps_sem, recv_sem=pr_sem,
            device_id=(g, a, b, s), device_id_type=MESH,
        )

    def total_of(buf, count, send_sem, recv_sem):
        part = buf.at[pl.ds(0, count)]
        return pltpu.make_async_remote_copy(
            src_ref=part, dst_ref=part, send_sem=send_sem, recv_sem=recv_sem,
            device_id=(g, v, t, other), device_id_type=MESH,
        )

    everyone(lambda to, p: exchange(to).start())
    total_of(sbuf, n - 1, ss_sem, sr_sem).wait_recv()

    def plane(c, i):
        x = sbuf[:, c * width + i // per, :]
        q = i % per
        return x if q == 0 else pltpu.roll(x, LANES - q * span, 1)

    own_row = lax.broadcasted_iota(jnp.int32, (n, LANES), 0) == me
    one_row = lax.broadcasted_iota(jnp.int32, (1, LANES), 1)
    square = lax.broadcasted_iota(jnp.int32, (LANES, LANES), 0)
    loss_here = jnp.zeros((1, 1), jnp.float32)
    columns = []
    for c in range(planes):
        at = [(plane(c, b), plane(c, here + b)) for b in range(here)]
        token_loss, grad_at, mass, norm = loss_planes(at, *(plane(c, 2 * here + i) for i in range(4)))
        mine = one_row + c * span == me
        loss_here = loss_here + jnp.sum(
            jnp.where(mine & (one_row < span), token_loss, 0.0), axis=1, keepdims=True
        )
        lines = [norm, mass] + [jnp.sum(jnp.where(own_row, x, 0.0), axis=0, keepdims=True) for x in grad_at]
        stacked = jnp.zeros((LANES, LANES), jnp.float32)
        for i, line in enumerate(lines):
            stacked = jnp.where(square == i, line, stacked)
        columns.append(stacked.T[:span])
    out_ref[ds_rows:, :] = jnp.broadcast_to(loss_here, (8, LANES))
    column = jnp.concatenate(columns, axis=0)
    norm, mass = column[:, 0:1], column[:, 1:2]
    logit_grad = -mass * jnp.exp(student - norm)
    added = [jnp.where(hits[b], column[:, 2 + b : 3 + b], 0.0) for b in range(here)]
    logit_grad = (logit_grad + jnp.concatenate(added, axis=1)).astype(jnp.bfloat16)

    step = 2 * LANES
    for j in range(0, ws.shape[0], step):
        product = lax.dot_general(
            logit_grad, ws[j : j + step, :], (((1,), (1,)), ((), ())), preferred_element_type=jnp.float32
        )
        for h in range(step // LANES):
            c = j // LANES + h
            ps[c * n : (c + 1) * n, :] = product[:, h * LANES : (h + 1) * LANES]

    def partial(p):
        return ps[pl.ds(p, ds_rows, stride=n), :].astype(jnp.bfloat16)

    def give(a):
        for b in range(T):
            pbuf[a * T + b] = partial(slot(a, b, other))
        to_pair(a).start()

    inward(give)
    give(v)

    def paired(a, b):
        return (partial(slot(a, b, s)).astype(jnp.float32) + rbuf[a * T + b].astype(jnp.float32)).astype(jnp.bfloat16)

    def pack(a):
        to_pair(a).wait_recv()
        for b in along:
            pbuf[chips + a * T + b] = paired(a, b)
            scatter(a, b).start()

    inward(pack)
    to_pair(v).wait_recv()
    for b in along[1:]:
        pbuf[chips + v * T + b] = paired(v, b)
        scatter(v, b).start()
    rbuf[chips + v * T + t] = paired(v, t)
    total_of(rbuf, chips - 1, ps_sem, pr_sem).wait_recv()

    def collect(q, total):
        return total + rbuf[chips + q].astype(jnp.float32)

    out_ref[:ds_rows, :] = lax.fori_loop(
        0, chips, collect, jnp.zeros((ds_rows, LANES), jnp.float32), unroll=8
    )

    outward(lambda a: to_z(a).wait_send())

    @pl.loop(0, V)
    def _(a):
        for d in range(1, T):
            to_xy(a, d).wait_send()
        for b in range(T):
            to_core(a, b).wait_send()

    total_of(sbuf, n - 1, ss_sem, sr_sem).wait_send()

    @pl.loop(0, V)
    def _(a):
        to_pair(a).wait_send()

    total_of(rbuf, chips - 1, ps_sem, pr_sem).wait_send()


def finish(out_ref, loss_ref, grad_ref):
    ds_rows = out_ref.shape[0] - 8
    for j in range(ds_rows):
        grad_ref[:, j * LANES : (j + 1) * LANES] = out_ref[j : j + 1, :].astype(jnp.bfloat16)
    loss_ref[...] = out_ref[ds_rows : ds_rows + 1, 0:1]


def local(sizes, student_hidden, teacher_hidden, student_head, teacher_head, proposed_block, proposed_offset):
    V, T, S = sizes
    n = V * T * S
    ds, width = student_head.shape
    dt = teacher_head.shape[0]
    ds_rows, dt_rows = ds // LANES, dt // LANES
    rows = ds_rows + dt_rows + 8
    K = proposed_block.shape[1]
    values = 2 * (width // BLK) + 4
    dma = pltpu.SemaphoreType.DMA
    result = pl.pallas_call(
        functools.partial(kernel, sizes),
        out_shape=jax.ShapeDtypeStruct((ds_rows + 8, LANES), jnp.float32),
        in_specs=[pl.BlockSpec(memory_space=pl.ANY)] * 6,
        out_specs=pl.BlockSpec(memory_space=pltpu.VMEM),
        scratch_shapes=[
            pltpu.VMEM((1, ds), jnp.bfloat16),
            pltpu.VMEM((1, dt), jnp.bfloat16),
            pltpu.VMEM((ds, width), jnp.bfloat16),
            pltpu.VMEM((dt, width), jnp.bfloat16),
            pltpu.VMEM((1, K), jnp.int32),
            pltpu.VMEM((1, K), jnp.int32),
            pltpu.VMEM((rows, LANES), jnp.float32),
            pltpu.VMEM((n, rows, LANES), jnp.bfloat16),
            pltpu.VMEM(((rows + 1) * n, LANES), jnp.float32),
            pltpu.VMEM((n, values * n // LANES, LANES), jnp.float32),
            pltpu.VMEM(((ds_rows + 1) * n, LANES), jnp.float32),
            pltpu.VMEM((n, ds_rows, LANES), jnp.bfloat16),
            pltpu.VMEM((n, ds_rows, LANES), jnp.bfloat16),
            dma((6,)),
            dma((V,)),
            dma((V, T)),
            dma((V, T)),
            dma((n,)),
            dma,
            dma,
            dma,
            dma,
            dma((V,)),
            dma((V,)),
        ],
        compiler_params=pltpu.CompilerParams(
            collective_id=0, has_side_effects=True, vmem_limit_bytes=56 * 1024 * 1024
        ),
        name="distill",
    )(student_hidden, teacher_hidden, student_head, teacher_head, proposed_block, proposed_offset)
    loss, grad = pl.pallas_call(
        finish,
        out_shape=(jax.ShapeDtypeStruct((1, 1), jnp.float32), jax.ShapeDtypeStruct((1, ds), jnp.bfloat16)),
        in_specs=[pl.BlockSpec(memory_space=pltpu.VMEM)],
        out_specs=(pl.BlockSpec(memory_space=pltpu.VMEM), pl.BlockSpec(memory_space=pltpu.VMEM)),
        compiler_params=pltpu.CompilerParams(vmem_limit_bytes=56 * 1024 * 1024),
        name="finish",
    )(result)
    return loss.reshape((1,)), grad


def solution(mesh):
    row = P(("groups", "vocab", "tokens", "sub"), None)
    return jax.shard_map(
        functools.partial(local, tuple(mesh.shape[a] for a in AXES)),
        mesh=mesh,
        in_specs=(row, row, P(None, AXES), P(None, AXES), row, row),
        out_specs=(P(("groups", "vocab", "tokens", "sub")), row),
        check_vma=False,
    )
```
